32 devices in a mesh: gx: 4 (over y, x), gy: 8 (over z, core).
Axes of the slice: x: 2, y: 2, z: 4, core: 2. Of those that a mesh axis runs over, the one named last changes fastest.
Arguments:
- densities: bfloat16 [16, 131072], P(None, ('gx', 'gy')), may hold values from -6 to 6
- points: float32 [3, 131072], P(None, ('gx', 'gy')), may hold values from 0 to 1
- weights: float32 [131072], P(('gx', 'gy')), may hold values from 0.03 to 0.6
- near_offsets: int32 [1024, 13], P(('gx', 'gy')), may hold values from -8 to 8, as said below
- leaf_basis: bfloat16 [1024, 64, 128], P(('gx', 'gy')), may hold values from -0.5 to 0.5
- transfer: bfloat16 [1024, 64, 64], P(('gx', 'gy')), may hold values from -0.75 to 0.75
- send_lists: int32 [32, 17, 16], P(('gx', 'gy')), may hold values from 0 to 31
- relay_refs: int32 [1024, 32], P(('gx', 'gy')), may hold values from 0 to 271, as said below
- leaf_coupling: bfloat16 [1024, 32, 64, 64], P(('gx', 'gy')), may hold values from -0.25 to 0.25
- coarse_refs: int32 [128, 32], P(('gx', 'gy')), may hold values from 0 to 127
- coarse_coupling: bfloat16 [128, 32, 64, 64], P(('gx', 'gy')), may hold values from -0.125 to 0.125
Outputs:
- potential: float32 [16, 131072], P(None, ('gx', 'gy'))
The draws below stay inside these ranges and needn't reach their ends.
Inputs may be any that keep to these rules, and one draw needn't show every extreme that they name: `near_offsets`: each leaf's offsets are distinct and the first is 0; a partner outside the leaves contributes nothing. `relay_refs`: a value never names an owner l // 32 + value // 16 - 8 outside 0 to 31; within the rows of each device's 32 leaves every other value is used at least once.
All inputs are finite; a program needn't handle non-finite values.
Results may differ from the reference program's by a relative error of at most 0.0065.
Values may be sent and summed in bfloat16 or wider, within the bound.
A program may use at most 128 MiB of HBM per device.

```python
import math
import jax
import jax.numpy as jnp
from jax import lax

RHS = 16
RANK = 64
LEAF_PTS = 128
LEAF_DEV = 32
NEAR = 13
REACH = 8
WINDOW = 8
FAR0 = 32
FAR1 = 32
LEAVES = 1024
POINTS = 131072
CLUSTERS = 128
CAPACITY = 16
N_GX = 4
N_GY = 8


def draw_near_offsets(key, part):

    def one_leaf(leaf_key):
        order = jax.random.permutation(leaf_key, 2 * REACH)
        picked = order[:NEAR - 1]
        shifted = jnp.where(picked < REACH, picked - REACH, picked - REACH + 1)
        return jnp.concatenate([jnp.zeros((1,), jnp.int32), shifted.astype(jnp.int32)])
    return jax.vmap(one_leaf)(jax.random.split(key, LEAVES)).astype(jnp.int32)


def draw_relay_refs(key, part):
    device_count = LEAVES // LEAF_DEV
    slot_total = (2 * WINDOW + 1) * CAPACITY
    total = LEAF_DEV * FAR0

    def one_device(device_index, device_key):
        bits_key, sign_key, slot_key, order_key = jax.random.split(device_key, 4)
        bits = jax.random.randint(bits_key, (total,), 0, 2 ** WINDOW)
        magnitude = jnp.zeros((total,), jnp.int32)
        for level in range(1, WINDOW + 1):
            magnitude = magnitude + (bits < 2 ** (WINDOW - level)).astype(jnp.int32)
        sign = jax.random.randint(sign_key, (total,), 0, 2) * 2 - 1
        offset = magnitude * sign
        owner = device_index + offset
        inside = (owner >= 0) & (owner < device_count)
        offset = jnp.where(inside, offset, -offset)
        slot = jax.random.randint(slot_key, (total,), 0, CAPACITY)
        extra = (offset + WINDOW) * CAPACITY + slot
        positions = jnp.arange(total, dtype=jnp.int32)
        cover = jnp.minimum(positions, slot_total - 1)
        cover_owner = device_index + cover // CAPACITY - WINDOW
        cover_fine = (positions < slot_total) & (cover_owner >= 0) & (cover_owner < device_count)
        mixed = jnp.where(cover_fine, cover, extra)
        return jax.random.permutation(order_key, mixed)
    blocks = jax.vmap(one_device)(jnp.arange(device_count, dtype=jnp.int32), jax.random.split(key, device_count))
    return blocks.reshape(LEAVES, FAR0).astype(jnp.int32)


def set_ends(entries, own_key, low, largest):
    longest = entries.shape.index(max(entries.shape))
    spots = []
    for shift in (0, 1):
        where = [jax.random.randint(jax.random.fold_in(own_key, axis), (), 0, length) for axis, length in enumerate(entries.shape)]
        where[longest] = (where[longest] + shift) % entries.shape[longest]
        spots.append(tuple(where))
    return entries.at[spots[0]].set(low).at[spots[1]].set(largest)


def block_scale(rng, extent, cuts, least, top_value):
    def one(position, shards_of):
        draws = jax.random.uniform(jax.random.fold_in(jax.random.fold_in(rng, 6), position), (shards_of,), jnp.float32, least / len(cuts), top_value / len(cuts))
        return jnp.repeat(jnp.exp(draws), extent[position] // shards_of).reshape((-1,) + (1,) * (len(extent) - position - 1))

    loudness = one(*cuts[0])
    for cut in cuts[1:]:
        loudness = loudness * one(*cut)
    return loudness


def normal_values(key, shape, spread, limit, cuts=(), kind=jnp.bfloat16):
    values = spread * jax.random.normal(key, shape, jnp.float32)
    if cuts:
        values = values * block_scale(key, shape, cuts, -0.22, 0.18)
    return jnp.clip(values, -limit, limit).astype(kind)


def setup_inputs(seed: int = 0) -> dict:
    streams_of = jax.random.split(jax.random.key(seed), 12)
    return {
        "densities": normal_values(streams_of[0], (RHS, POINTS), 1.0, 6.0, ((1, 32),)),
        "points": jnp.clip(1.0 * jax.random.uniform(streams_of[1], (3, POINTS), jnp.float32) ** block_scale(streams_of[1], (3, POINTS), ((1, 32),), -0.2, 0.2), 0.0, 1.0),
        "weights": jnp.clip(jnp.exp(math.log(0.6) - 2.9957323 * jax.random.uniform(streams_of[2], (POINTS,), jnp.float32) ** block_scale(streams_of[2], (POINTS,), ((0, 32),), -0.2, 0.2)), 0.03, 0.6),
        "near_offsets": draw_near_offsets(jax.random.fold_in(streams_of[11], 71), 0),
        "leaf_basis": normal_values(streams_of[4], (LEAVES, RANK, LEAF_PTS), LEAF_PTS ** -0.5, 0.5, ((0, 32),)),
        "transfer": normal_values(streams_of[5], (LEAVES, RANK, RANK), RANK ** -0.5, 0.75, ((0, 32),)),
        "send_lists": set_ends(jax.random.randint(streams_of[6], (N_GX * N_GY, 2 * WINDOW + 1, CAPACITY), 0, LEAF_DEV), jax.random.fold_in(streams_of[6], 1), 0, LEAF_DEV - 1).astype(jnp.int32),
        "relay_refs": draw_relay_refs(jax.random.fold_in(streams_of[11], 71), 0),
        "leaf_coupling": normal_values(streams_of[8], (LEAVES, FAR0, RANK, RANK), (RANK * FAR0 // 4) ** -0.5, 0.25, ((0, 32),)),
        "coarse_refs": set_ends(jax.random.randint(streams_of[9], (CLUSTERS, FAR1), 0, CLUSTERS), jax.random.fold_in(streams_of[9], 1), 0, CLUSTERS - 1).astype(jnp.int32),
        "coarse_coupling": normal_values(streams_of[10], (CLUSTERS, FAR1, RANK, RANK), (RANK * FAR1) ** -0.5, 0.125, ((0, 32),)),
    }


core_square = 0.0004
four_pi = 4.0 * math.pi

def near_field(densities, points, weights, near_offsets):
    rim_cells = REACH * LEAF_PTS
    packed = jnp.concatenate([densities.astype(jnp.float32), points, weights[None, :]], axis=0)
    padded = jnp.pad(packed, ((0, 0), (rim_cells, rim_cells)))
    extended = padded.reshape(RHS + 4, LEAVES + 2 * REACH, LEAF_PTS)
    row_points = points.reshape(3, LEAVES, LEAF_PTS)
    partners = (jnp.arange(LEAVES, dtype=jnp.int32)[:, None] + REACH + near_offsets).astype(jnp.int32)

    def near_block(block_index):
        partner_rows = lax.dynamic_slice_in_dim(partners, block_index * 8, 8, 0)
        partner_data = jnp.take(extended, partner_rows, axis=1)
        own_points = lax.dynamic_slice_in_dim(row_points, block_index * 8, 8, 1)
        distance = jnp.zeros((8, LEAF_PTS, NEAR, LEAF_PTS), jnp.float32)
        for component in range(3):
            offset_part = own_points[component][:, :, None, None] - partner_data[RHS + component][:, None, :, :]
            distance = distance + offset_part * offset_part
        kernel = (partner_data[RHS + 3][:, None, :, :] / (four_pi * jnp.sqrt(distance + core_square))).astype(jnp.bfloat16)
        partner_values = partner_data[:RHS].astype(jnp.bfloat16)
        return jnp.einsum('lisj,rlsj->rli', kernel.astype(jnp.float32), partner_values.astype(jnp.float32))
    blocks_out = lax.map(near_block, jnp.arange(LEAVES // 8, dtype=jnp.int32))
    return jnp.transpose(blocks_out, (1, 0, 2, 3)).reshape(RHS, POINTS)

def reference(densities, points, weights, near_offsets, leaf_basis, transfer, send_lists, relay_refs, leaf_coupling, coarse_refs, coarse_coupling):
    values = densities.astype(jnp.float32).reshape(RHS, LEAVES, LEAF_PTS)
    basis_wide = leaf_basis.astype(jnp.float32)
    coeff0 = jnp.einsum('lkm,rlm->lrk', basis_wide, values).astype(jnp.bfloat16)
    device_count = LEAVES // LEAF_DEV

    def relay_block(device_index):
        refs_block = lax.dynamic_slice_in_dim(relay_refs, device_index * LEAF_DEV, LEAF_DEV, 0)
        window_index = (refs_block // CAPACITY).astype(jnp.int32)
        slot_index = (refs_block % CAPACITY).astype(jnp.int32)
        source = jnp.clip(device_index + window_index - WINDOW, 0, device_count - 1).astype(jnp.int32)
        chosen = send_lists[source, 2 * WINDOW - window_index, slot_index]
        column = (source * LEAF_DEV + chosen).astype(jnp.int32)
        picked = jnp.take(coeff0, column, axis=0).astype(jnp.float32)
        coupling = lax.dynamic_slice_in_dim(leaf_coupling, device_index * LEAF_DEV, LEAF_DEV, 0).astype(jnp.float32)
        return jnp.einsum('lsab,lsrb->lra', coupling, picked)
    local0 = lax.map(relay_block, jnp.arange(device_count, dtype=jnp.int32)).reshape(LEAVES, RHS, RANK)
    transfer_wide = transfer.astype(jnp.float32).reshape(CLUSTERS, 8, RANK, RANK)
    coeff1 = jnp.einsum('qcab,qcra->qrb', transfer_wide, coeff0.astype(jnp.float32).reshape(CLUSTERS, 8, RHS, RANK)).astype(jnp.bfloat16)
    coarse_picked = jnp.take(coeff1, coarse_refs, axis=0).astype(jnp.float32)
    local1 = jnp.einsum('qsab,qsrb->qra', coarse_coupling.astype(jnp.float32), coarse_picked).astype(jnp.bfloat16)
    downward = jnp.einsum('qcab,qrb->qcra', transfer_wide, local1.astype(jnp.float32)).reshape(LEAVES, RHS, RANK)
    leaf_field = (local0 + downward).astype(jnp.bfloat16)
    far_field = jnp.einsum('lkm,lrk->rlm', basis_wide, leaf_field.astype(jnp.float32)).reshape(RHS, POINTS)
    return far_field + near_field(densities, points, weights, near_offsets)
```

```python
import functools
import math

import jax
import jax.numpy as jnp
from jax import lax
from jax.experimental import pallas as pl
from jax.experimental.pallas import tpu as pltpu
from jax.sharding import PartitionSpec as P

REACH = 8
WINDOW = 8
CHILDREN = 8
WINDOWS = 2 * WINDOW + 1

core_square = 0.0004
four_pi = 4.0 * math.pi

MESH = pl.DeviceIdType.MESH
ROWS_BY_ROWS = (((1,), (1,)), ((), ()))
PLAIN = (((1,), (0,)), ((), ()))


def dot(left, right, dims):
    return lax.dot_general(left, right, dims, preferred_element_type=jnp.float32)


def split(values):
    first = values.astype(jnp.bfloat16).astype(jnp.float32)
    rest = values - first
    second = rest.astype(jnp.bfloat16).astype(jnp.float32)
    return first, second, rest - second


def features(pack):
    row = lax.broadcasted_iota(jnp.int32, pack.shape, 0)
    shifted = pack - 0.5
    squares = shifted * shifted
    norm = squares[0:1] + squares[1:2] + squares[2:3]
    root = four_pi / pack[3:4]
    scale = root * root
    left = jnp.where(row < 3, shifted, jnp.where(row == 3, norm, jnp.where(row == 4, 1.0, 0.0)))
    right = scale * jnp.where(
        row < 3,
        -2.0 * shifted,
        jnp.where(row == 3, 1.0, jnp.where(row == 4, norm + core_square, 0.0)),
    )
    a1, a2, a3 = split(left)
    b1, b2, b3 = split(right)
    return (
        jnp.concatenate([a1, a1, a2, a1, a3, a2], axis=0),
        jnp.concatenate([b1, b2, b1, b3, b1, b2], axis=0),
    )


def exchange_kernel(
    sizes,
    offsets_ref,
    lists_ref,
    dens_ref,
    pack_ref,
    basis_ref,
    transfer_ref,
    near_ref,
    listed_ref,
    coarse_ref,
    row_feat,
    col_feat,
    values,
    coeff,
    outgoing,
    halo_dens,
    halo_pack,
    halo_send,
    halo_recv,
    list_send,
    list_recv,
    coarse_send,
    coarse_recv,
):
    n_gx, n_gy = sizes
    total = n_gx * n_gy
    me = lax.axis_index("gx") * n_gy + lax.axis_index("gy")
    leaf_count, rank, leaf_size = basis_ref.shape
    slots = offsets_ref.shape[1]
    groups = leaf_count // CHILDREN
    half_slots = lists_ref.shape[1] // 2
    rim = REACH * leaf_size
    columns = leaf_count * leaf_size

    def place(index):
        return (index // n_gy, index % n_gy)

    barrier = pltpu.get_barrier_semaphore()

    def greet(step, carry):
        other = (me + step) % total
        pl.semaphore_signal(barrier, inc=1, device_id=place(other), device_id_type=MESH)
        return carry

    lax.fori_loop(1, total, greet, 0)

    low = lax.broadcasted_iota(jnp.int32, (dens_ref.shape[0], 2 * rank), 1) < rank

    def upward(pair, carry):
        parents = []
        for g in range(2):
            parent = None
            for child in range(CHILDREN):
                leaf = (pair * 2 + g) * CHILDREN + child
                start = pl.multiple_of(leaf * leaf_size, leaf_size)
                basis = basis_ref[leaf]
                doubled = jnp.concatenate([basis, basis], axis=0)
                both = dot(dens_ref[:, pl.ds(start, leaf_size)], doubled, ROWS_BY_ROWS)
                both = both.astype(jnp.bfloat16)
                coeff[leaf] = both
                term = dot(both[:, :rank], transfer_ref[leaf], PLAIN)
                parent = term if parent is None else parent + term
            parents.append(parent)
        coarse_ref[me, pair] = jnp.concatenate(parents, axis=1).astype(jnp.bfloat16)
        return carry

    lax.fori_loop(0, groups // 2, upward, 0)

    def gather(window, carry):
        for slot in range(half_slots):
            first = coeff[lists_ref[window, slot]]
            second = coeff[lists_ref[window, slot + half_slots]]
            outgoing[window, slot] = jnp.where(low, first, second)
        return carry

    lax.fori_loop(0, WINDOWS, gather, 0)
    listed_ref[WINDOW] = outgoing[WINDOW]

    pl.semaphore_wait(barrier, total - 1)

    def halo(side):
        other = place(me - 1 if side == 0 else me + 1)
        start = 0 if side == 0 else columns - rim
        return [
            pltpu.make_async_remote_copy(
                src_ref=source.at[:, pl.ds(start, rim)],
                dst_ref=target.at[1 - side],
                send_sem=halo_send.at[side, kind],
                recv_sem=halo_recv.at[1 - side, kind],
                device_id=other,
                device_id_type=MESH,
            )
            for kind, (source, target) in enumerate([(dens_ref, halo_dens), (pack_ref, halo_pack)])
        ]

    @pl.when(me > 0)
    def _():
        for copy in halo(0):
            copy.start()

    @pl.when(me < total - 1)
    def _():
        for copy in halo(1):
            copy.start()

    def coarse_copy(other, slot):
        return pltpu.make_async_remote_copy(
            src_ref=coarse_ref.at[slot],
            dst_ref=coarse_ref.at[slot],
            send_sem=coarse_send.at[other],
            recv_sem=coarse_recv.at[slot],
            device_id=place(other),
            device_id_type=MESH,
        )

    def list_copy(window, landing):
        return pltpu.make_async_remote_copy(
            src_ref=outgoing.at[window],
            dst_ref=listed_ref.at[landing],
            send_sem=list_send.at[window],
            recv_sem=list_recv.at[landing],
            device_id=place(me + window - WINDOW),
            device_id_type=MESH,
        )

    def in_window(window):
        other = me + window - WINDOW
        return (window != WINDOW) & (other >= 0) & (other < total)

    def send_list(window, carry):
        @pl.when(in_window(window))
        def _():
            list_copy(window, 2 * WINDOW - window).start()

        return carry

    def send_coarse(step, carry):
        coarse_copy((me + step) % total, me).start()
        return carry

    lax.fori_loop(1, total, send_coarse, 0)
    lax.fori_loop(0, WINDOWS, send_list, 0)

    batch = 4

    def prepare(first_leaf, pack, dens, own):
        left, right = features(pack)
        right = right.astype(jnp.bfloat16)
        for k in range(batch):
            part = slice(k * leaf_size, (k + 1) * leaf_size)
            col_feat[first_leaf + k] = right[:, part]
            values[first_leaf + k] = dens[:, part]
            if own:
                row_feat[first_leaf - REACH + k] = left[:, part].T.astype(jnp.bfloat16)

    def prepare_own(step, carry):
        span = pl.ds(pl.multiple_of(step * batch * leaf_size, batch * leaf_size), batch * leaf_size)
        prepare(REACH + step * batch, pack_ref[:, span], dens_ref[:, span], True)
        return carry

    lax.fori_loop(0, leaf_count // batch, prepare_own, 0)

    def near_leaf(leaf, carry):
        mine = row_feat[leaf]
        field = jnp.zeros((dens_ref.shape[0], leaf_size), jnp.float32)
        partners = [leaf + REACH + offsets_ref[leaf, slot] for slot in range(slots)]
        for first in range(0, slots, 2):
            some = partners[first : first + 2]
            cols = jnp.concatenate([col_feat[p] for p in some], axis=1)
            vals = jnp.concatenate([values[p] for p in some], axis=1)
            kernel = lax.rsqrt(dot(mine, cols, PLAIN)).astype(jnp.bfloat16)
            field = field + dot(vals, kernel, ROWS_BY_ROWS)
        near_ref[:, pl.ds(pl.multiple_of(leaf * leaf_size, leaf_size), leaf_size)] = field
        return carry

    lax.fori_loop(REACH, leaf_count - REACH, near_leaf, 0)

    @pl.when(me == 0)
    def _():
        halo_dens[0] = jnp.zeros(halo_dens.shape[1:], halo_dens.dtype)
        halo_pack[0] = jnp.ones(halo_pack.shape[1:], halo_pack.dtype)

    @pl.when(me == total - 1)
    def _():
        halo_dens[1] = jnp.zeros(halo_dens.shape[1:], halo_dens.dtype)
        halo_pack[1] = jnp.ones(halo_pack.shape[1:], halo_pack.dtype)

    @pl.when(me > 0)
    def _():
        for copy in halo(1):
            copy.wait_recv()
        for copy in halo(0):
            copy.wait_send()

    @pl.when(me < total - 1)
    def _():
        for copy in halo(0):
            copy.wait_recv()
        for copy in halo(1):
            copy.wait_send()

    for side in range(2):
        base = 0 if side == 0 else REACH + leaf_count

        def prepare_rim(step, carry, side=side, base=base):
            width = batch * leaf_size
            span = pl.ds(pl.multiple_of(step * width, width), width)
            prepare(base + step * batch, halo_pack[side, :, span], halo_dens[side, :, span], False)
            return carry

        lax.fori_loop(0, REACH // batch, prepare_rim, 0)

    lax.fori_loop(0, REACH, near_leaf, 0)
    lax.fori_loop(leaf_count - REACH, leaf_count, near_leaf, 0)

    def end_coarse(step, carry):
        other = (me + step) % total
        coarse_copy(other, other).wait_recv()
        coarse_copy(other, me).wait_send()
        return carry

    lax.fori_loop(1, total, end_coarse, 0)

    def end_list(window, carry):
        @pl.when(in_window(window))
        def _():
            list_copy(window, window).wait_recv()
            list_copy(window, 2 * WINDOW - window).wait_send()

        return carry

    lax.fori_loop(0, WINDOWS, end_list, 0)


def exchange(sizes, offsets, lists, densities, pack, leaf_basis, transfer):
    rhs, columns = densities.shape
    leaf_count, rank, leaf_size = leaf_basis.shape
    total = sizes[0] * sizes[1]
    groups = leaf_count // CHILDREN
    half_slots = lists.shape[1] // 2
    vmem = pl.BlockSpec(memory_space=pltpu.VMEM)
    smem = pl.BlockSpec(memory_space=pltpu.SMEM)
    rim = REACH * leaf_size
    dma = pltpu.SemaphoreType.DMA
    return pl.pallas_call(
        functools.partial(exchange_kernel, sizes),
        out_shape=(
            jax.ShapeDtypeStruct((rhs, columns), jnp.float32),
            jax.ShapeDtypeStruct((WINDOWS, half_slots, rhs, 2 * rank), jnp.bfloat16),
            jax.ShapeDtypeStruct((total, groups // 2, rhs, 2 * rank), jnp.bfloat16),
        ),
        in_specs=[smem, smem, vmem, vmem, vmem, vmem],
        out_specs=(vmem, vmem, vmem),
        scratch_shapes=[
            pltpu.VMEM((leaf_count, leaf_size, 48), jnp.bfloat16),
            pltpu.VMEM((leaf_count + 2 * REACH, 48, leaf_size), jnp.bfloat16),
            pltpu.VMEM((leaf_count + 2 * REACH, rhs, leaf_size), jnp.bfloat16),
            pltpu.VMEM((leaf_count, rhs, 2 * rank), jnp.bfloat16),
            pltpu.VMEM((WINDOWS, half_slots, rhs, 2 * rank), jnp.bfloat16),
            pltpu.VMEM((2, rhs, rim), jnp.bfloat16),
            pltpu.VMEM((2, 8, rim), jnp.float32),
            dma((2, 2)),
            dma((2, 2)),
            dma((WINDOWS,)),
            dma((WINDOWS,)),
            dma((total,)),
            dma((total,)),
        ],
        compiler_params=pltpu.CompilerParams(
            collective_id=0, has_side_effects=True, vmem_limit_bytes=32 * 1024 * 1024
        ),
        name="exchange",
    )(offsets, lists, densities, pack, leaf_basis, transfer)


def far_kernel(
    relay_ref,
    refs_ref,
    listed_ref,
    coarse_ref,
    coupling_ref,
    coarse_coupling_ref,
    transfer_ref,
    basis_ref,
    near_ref,
    out_ref,
    listed,
    coarse,
):
    step = pl.program_id(0)
    rank, leaf_size = basis_ref.shape[1:]
    rhs = near_ref.shape[0]
    low = lax.broadcasted_iota(jnp.int32, (rhs, 2 * rank), 1) < rank

    @pl.when(step == 0)
    def _():
        half = listed_ref.shape[1]

        def open_list(window, carry):
            for slot in range(half):
                both = listed_ref[window, slot].astype(jnp.float32)
                turned = pltpu.roll(both, rank, 1)
                index = window * 2 * half + slot
                listed[index] = jnp.where(low, both, turned).astype(jnp.bfloat16)
                listed[index + half] = jnp.where(low, turned, both).astype(jnp.bfloat16)
            return carry

        lax.fori_loop(0, listed_ref.shape[0], open_list, 0)
        pairs = coarse_ref.shape[1]

        def open_coarse(owner, carry):
            for k in range(4 * pairs):
                both = coarse_ref[owner * 4 + k // pairs, k % pairs].astype(jnp.float32)
                turned = pltpu.roll(both, rank, 1)
                index = owner * 8 * pairs + 2 * k
                coarse[index] = jnp.where(low, both, turned).astype(jnp.bfloat16)
                coarse[index + 1] = jnp.where(low, turned, both).astype(jnp.bfloat16)
            return carry

        lax.fori_loop(0, coarse_ref.shape[0] // 4, open_coarse, 0)

    def couple(blocks, store, pick, count):
        total = jnp.zeros((rhs, rank), jnp.float32)
        for slot in range(0, count, 4):
            matrix = jnp.concatenate([blocks(slot + k) for k in range(4)], axis=1)
            taken = [store[pick(slot + k)] for k in range(4)]
            picked = jnp.concatenate(
                [jnp.where(low, taken[0], taken[1]), jnp.where(low, taken[2], taken[3])], axis=1
            )
            total = total + dot(picked, matrix, ROWS_BY_ROWS)
        return total

    local1 = couple(
        lambda s: coarse_coupling_ref[0, s], coarse, lambda s: refs_ref[step, s], refs_ref.shape[1]
    ).astype(jnp.bfloat16)

    def one_leaf(child, carry):
        leaf = step * CHILDREN + child
        local0 = couple(
            lambda s: coupling_ref[child, s], listed, lambda s: relay_ref[leaf, s], relay_ref.shape[1]
        )
        downward = dot(local1, transfer_ref[child], ROWS_BY_ROWS)
        field = (local0 + downward).astype(jnp.bfloat16)
        span = pl.ds(pl.multiple_of(child * leaf_size, leaf_size), leaf_size)
        out_ref[:, span] = near_ref[:, span] + dot(field, basis_ref[child], PLAIN)
        return carry

    lax.fori_loop(0, CHILDREN, one_leaf, 0, unroll=2)


def far(relay_refs, coarse_refs, listed, everyone, coupling, coarse_coupling, transfer, basis, near):
    leaf_count, rank, leaf_size = basis.shape
    rhs = near.shape[0]
    groups = leaf_count // CHILDREN
    width = CHILDREN * leaf_size
    vmem = pl.BlockSpec(memory_space=pltpu.VMEM)
    smem = pl.BlockSpec(memory_space=pltpu.SMEM)
    return pl.pallas_call(
        far_kernel,
        grid=(groups,),
        out_shape=jax.ShapeDtypeStruct(near.shape, jnp.float32),
        in_specs=[
            smem,
            smem,
            vmem,
            vmem,
            pl.BlockSpec((CHILDREN,) + coupling.shape[1:], lambda q: (q, 0, 0, 0)),
            pl.BlockSpec((1,) + coarse_coupling.shape[1:], lambda q: (q, 0, 0, 0)),
            pl.BlockSpec((CHILDREN, rank, rank), lambda q: (q, 0, 0)),
            pl.BlockSpec((CHILDREN, rank, leaf_size), lambda q: (q, 0, 0)),
            pl.BlockSpec((rhs, width), lambda q: (0, q)),
        ],
        out_specs=pl.BlockSpec((rhs, width), lambda q: (0, q)),
        scratch_shapes=[
            pltpu.VMEM((listed.shape[0] * listed.shape[1] * 2, rhs, 2 * rank), jnp.bfloat16),
            pltpu.VMEM((everyone.shape[0] * everyone.shape[1] * 2, rhs, 2 * rank), jnp.bfloat16),
        ],
        compiler_params=pltpu.CompilerParams(vmem_limit_bytes=40 * 1024 * 1024),
        name="far",
    )(relay_refs, coarse_refs, listed, everyone, coupling, coarse_coupling, transfer, basis, near)


def local(
    sizes,
    densities,
    points,
    weights,
    near_offsets,
    leaf_basis,
    transfer,
    send_lists,
    relay_refs,
    leaf_coupling,
    coarse_refs,
    coarse_coupling,
):
    pack = jnp.concatenate([points, jnp.broadcast_to(weights[None, :], (5, weights.shape[0]))], axis=0)
    near, listed, everyone = exchange(
        sizes, near_offsets, send_lists[0], densities, pack, leaf_basis, transfer
    )
    return far(
        relay_refs,
        coarse_refs,
        listed,
        everyone,
        leaf_coupling,
        coarse_coupling,
        transfer,
        leaf_basis,
        near,
    )


def solution(mesh):
    sizes = (mesh.shape["gx"], mesh.shape["gy"])
    in_specs = (
        P(None, ("gx", "gy")),
        P(None, ("gx", "gy")),
        P(("gx", "gy")),
        P(("gx", "gy"), None),
        P(("gx", "gy"), None, None),
        P(("gx", "gy"), None, None),
        P(("gx", "gy"), None, None),
        P(("gx", "gy"), None),
        P(("gx", "gy"), None, None, None),
        P(("gx", "gy"), None),
        P(("gx", "gy"), None, None, None),
    )
    out_specs = P(None, ("gx", "gy"))
    return jax.shard_map(
        functools.partial(local, sizes),
        mesh=mesh,
        in_specs=in_specs,
        out_specs=out_specs,
        check_vma=False,
    )
```

```python
import functools
import math

import jax
import jax.numpy as jnp
from jax import lax
from jax.experimental import pallas as pl
from jax.experimental.pallas import tpu as pltpu
from jax.sharding import PartitionSpec as P

REACH = 8
WINDOW = 8
CHILDREN = 8
WINDOWS = 2 * WINDOW + 1

core_square = 0.0004
four_pi = 4.0 * math.pi

MESH = pl.DeviceIdType.MESH
ROWS_BY_ROWS = (((1,), (1,)), ((), ()))
PLAIN = (((1,), (0,)), ((), ()))


def dot(left, right, dims):
    return lax.dot_general(left, right, dims, preferred_element_type=jnp.float32)


def split(values):
    first = values.astype(jnp.bfloat16).astype(jnp.float32)
    rest = values - first
    second = rest.astype(jnp.bfloat16).astype(jnp.float32)
    return first, second, rest - second


def features(points, weights):
    row = lax.broadcasted_iota(jnp.int32, (8, points.shape[1]), 0)
    x, y, z = (points[k : k + 1] - 0.5 for k in range(3))
    norm = x * x + y * y + z * z
    root = four_pi / weights
    scale = root * root
    shifted = jnp.where(row == 0, x, jnp.where(row == 1, y, z))
    left = jnp.where(row < 3, shifted, jnp.where(row == 3, norm, jnp.where(row == 4, 1.0, 0.0)))
    right = scale * jnp.where(
        row < 3,
        -2.0 * shifted,
        jnp.where(row == 3, 1.0, jnp.where(row == 4, norm + core_square, 0.0)),
    )
    a1, a2, a3 = split(left)
    b1, b2, b3 = split(right)
    return (
        jnp.concatenate([a1, a1, a2, a1, a3, a2], axis=0),
        jnp.concatenate([b1, b2, b1, b3, b1, b2], axis=0),
    )


def whole_kernel(
    sizes,
    spans,
    table_ref,
    dens_any,
    points_any,
    weights_any,
    basis_any,
    transfer_any,
    coarse_coupling_any,
    coupling_any,
    out_ref,
    dens_ref,
    points_ref,
    weights_ref,
    basis_ref,
    transfer_ref,
    coarse_coupling_ref,
    coupling_ref,
    row_feat,
    col_feat,
    values,
    coeff,
    outgoing,
    listed_packed,
    coarse_packed,
    listed,
    coarse,
    local1,
    halo_dens,
    halo_points,
    halo_weights,
    load_sems,
    coupling_sems,
    halo_send,
    halo_recv,
    list_send,
    list_recv,
    coarse_send,
    coarse_recv,
):
    n_gx, n_gy = sizes
    total = n_gx * n_gy
    me = lax.axis_index("gx") * n_gy + lax.axis_index("gy")
    leaf_count, rank, leaf_size = basis_ref.shape
    rhs = dens_ref.shape[0]
    slots, far0, capacity, far1 = spans
    at_lists = slots
    at_relay = at_lists + capacity
    at_coarse = at_relay + leaf_count
    groups = leaf_count // CHILDREN
    half_slots = capacity // 2
    rim = REACH * leaf_size
    columns = leaf_count * leaf_size

    loads = [
        pltpu.make_async_copy(source, target, load_sems.at[k])
        for k, (source, target) in enumerate(
            [
                (dens_any, dens_ref),
                (basis_any, basis_ref),
                (transfer_any, transfer_ref),
                (points_any, points_ref),
                (weights_any, weights_ref),
                (coarse_coupling_any, coarse_coupling_ref),
            ]
        )
    ]
    for load in loads:
        load.start()

    def coupling_load(group):
        span = pl.ds(group * CHILDREN, CHILDREN)
        return pltpu.make_async_copy(
            coupling_any.at[span], coupling_ref.at[span], coupling_sems.at[group]
        )

    for group in range(groups):
        coupling_load(group).start()

    def place(index):
        return (index // n_gy, index % n_gy)

    barrier = pltpu.get_barrier_semaphore()

    def greet(step, carry):
        other = (me + step) % total
        pl.semaphore_signal(barrier, inc=1, device_id=place(other), device_id_type=MESH)
        return carry

    lax.fori_loop(1, total, greet, 0)
    for load in loads[:3]:
        load.wait()

    low = lax.broadcasted_iota(jnp.int32, (rhs, 2 * rank), 1) < rank

    def upward(pair, carry):
        parents = []
        for g in range(2):
            parent = None
            for child in range(CHILDREN):
                leaf = (pair * 2 + g) * CHILDREN + child
                start = pl.multiple_of(leaf * leaf_size, leaf_size)
                basis = basis_ref[leaf]
                doubled = jnp.concatenate([basis, basis], axis=0)
                both = dot(dens_ref[:, pl.ds(start, leaf_size)], doubled, ROWS_BY_ROWS)
                both = both.astype(jnp.bfloat16)
                coeff[leaf] = both
                term = dot(both[:, :rank], transfer_ref[leaf], PLAIN)
                parent = term if parent is None else parent + term
            parents.append(parent)
        coarse_packed[me, pair] = jnp.concatenate(parents, axis=1).astype(jnp.bfloat16)
        return carry

    lax.fori_loop(0, groups // 2, upward, 0)

    def gather(window, carry):
        for slot in range(half_slots):
            first = coeff[table_ref[at_lists + slot, window]]
            second = coeff[table_ref[at_lists + slot + half_slots, window]]
            outgoing[window, slot] = jnp.where(low, first, second)
        return carry

    lax.fori_loop(0, WINDOWS, gather, 0)
    listed_packed[WINDOW] = outgoing[WINDOW]
    loads[3].wait()
    loads[4].wait()

    pl.semaphore_wait(barrier, total - 1)

    def halo(side):
        other = place(me - 1 if side == 0 else me + 1)
        start = 0 if side == 0 else columns - rim
        leaf = 0 if side == 0 else leaf_count - REACH
        parts = [
            (dens_ref.at[:, pl.ds(start, rim)], halo_dens),
            (points_ref.at[:, pl.ds(start, rim)], halo_points),
            (weights_ref.at[pl.ds(leaf, REACH)], halo_weights),
        ]
        return [
            pltpu.make_async_remote_copy(
                src_ref=source,
                dst_ref=target.at[1 - side],
                send_sem=halo_send.at[side, kind],
                recv_sem=halo_recv.at[1 - side, kind],
                device_id=other,
                device_id_type=MESH,
            )
            for kind, (source, target) in enumerate(parts)
        ]

    @pl.when(me > 0)
    def _():
        for copy in halo(0):
            copy.start()

    @pl.when(me < total - 1)
    def _():
        for copy in halo(1):
            copy.start()

    def coarse_copy(other, slot):
        return pltpu.make_async_remote_copy(
            src_ref=coarse_packed.at[slot],
            dst_ref=coarse_packed.at[slot],
            send_sem=coarse_send.at[other],
            recv_sem=coarse_recv.at[slot],
            device_id=place(other),
            device_id_type=MESH,
        )

    def list_copy(window, landing):
        return pltpu.make_async_remote_copy(
            src_ref=outgoing.at[window],
            dst_ref=listed_packed.at[landing],
            send_sem=list_send.at[window],
            recv_sem=list_recv.at[landing],
            device_id=place(me + window - WINDOW),
            device_id_type=MESH,
        )

    def in_window(window):
        other = me + window - WINDOW
        return (window != WINDOW) & (other >= 0) & (other < total)

    def send_list(window, carry):
        @pl.when(in_window(window))
        def _():
            list_copy(window, 2 * WINDOW - window).start()

        return carry

    def send_coarse(step, carry):
        coarse_copy((me + step) % total, me).start()
        return carry

    lax.fori_loop(1, total, send_coarse, 0)
    lax.fori_loop(0, WINDOWS, send_list, 0)

    batch = 4

    def prepare(first_leaf, points, weights, dens, own):
        line = jnp.concatenate([weights[k : k + 1] for k in range(batch)], axis=1)
        left, right = features(points, line)
        right = right.astype(jnp.bfloat16)
        for k in range(batch):
            part = slice(k * leaf_size, (k + 1) * leaf_size)
            col_feat[first_leaf + k] = right[:, part]
            values[first_leaf + k] = dens[:, part]
            if own:
                row_feat[first_leaf - REACH + k] = left[:, part].T.astype(jnp.bfloat16)

    def prepare_own(step, carry):
        span = pl.ds(pl.multiple_of(step * batch * leaf_size, batch * leaf_size), batch * leaf_size)
        lines = weights_ref[pl.ds(step * batch, batch)]
        prepare(REACH + step * batch, points_ref[:, span], lines, dens_ref[:, span], True)
        return carry

    lax.fori_loop(0, leaf_count // batch, prepare_own, 0)

    def near_leaf(leaf, carry):
        mine = row_feat[leaf]
        field = jnp.zeros((leaf_size, rhs), jnp.float32)
        partners = [leaf + REACH + table_ref[slot, leaf] for slot in range(slots)]
        for first in range(0, slots, 2):
            some = partners[first : first + 2]
            cols = jnp.concatenate([col_feat[p] for p in some], axis=1)
            vals = jnp.concatenate([values[p] for p in some], axis=1)
            kernel = lax.rsqrt(dot(mine, cols, PLAIN)).astype(jnp.bfloat16)
            field = field + dot(kernel, vals, ROWS_BY_ROWS)
        out_ref[:, pl.ds(pl.multiple_of(leaf * leaf_size, leaf_size), leaf_size)] = field.T
        return carry

    lax.fori_loop(REACH, leaf_count - REACH, near_leaf, 0)

    @pl.when(me == 0)
    def _():
        halo_dens[0] = jnp.zeros(halo_dens.shape[1:], halo_dens.dtype)
        halo_points[0] = jnp.zeros(halo_points.shape[1:], halo_points.dtype)
        halo_weights[0] = jnp.ones(halo_weights.shape[1:], halo_weights.dtype)

    @pl.when(me == total - 1)
    def _():
        halo_dens[1] = jnp.zeros(halo_dens.shape[1:], halo_dens.dtype)
        halo_points[1] = jnp.zeros(halo_points.shape[1:], halo_points.dtype)
        halo_weights[1] = jnp.ones(halo_weights.shape[1:], halo_weights.dtype)

    @pl.when(me > 0)
    def _():
        for copy in halo(1):
            copy.wait_recv()
        for copy in halo(0):
            copy.wait_send()

    @pl.when(me < total - 1)
    def _():
        for copy in halo(0):
            copy.wait_recv()
        for copy in halo(1):
            copy.wait_send()

    for side in range(2):
        base = 0 if side == 0 else REACH + leaf_count

        def prepare_rim(step, carry, side=side, base=base):
            width = batch * leaf_size
            span = pl.ds(pl.multiple_of(step * width, width), width)
            lines = halo_weights[side, pl.ds(step * batch, batch)]
            dens = halo_dens[side, :, span]
            prepare(base + step * batch, halo_points[side, :, span], lines, dens, False)
            return carry

        lax.fori_loop(0, REACH // batch, prepare_rim, 0)

    lax.fori_loop(0, REACH, near_leaf, 0)
    lax.fori_loop(leaf_count - REACH, leaf_count, near_leaf, 0)

    def end_coarse(step, carry):
        other = (me + step) % total
        coarse_copy(other, other).wait_recv()
        coarse_copy(other, me).wait_send()
        return carry

    lax.fori_loop(1, total, end_coarse, 0)

    def opened(packed):
        both = packed.astype(jnp.float32)
        turned = pltpu.roll(both, rank, 1)
        return (
            jnp.where(low, both, turned).astype(jnp.bfloat16),
            jnp.where(low, turned, both).astype(jnp.bfloat16),
        )

    pairs = groups // 2

    def open_coarse(step, carry):
        for k in range(4 * pairs):
            first, second = opened(coarse_packed[step * 4 + k // pairs, k % pairs])
            index = step * 8 * pairs + 2 * k
            coarse[index] = first
            coarse[index + 1] = second
        return carry

    lax.fori_loop(0, total // 4, open_coarse, 0)
    loads[5].wait()

    def couple(blocks, store, pick, count):
        field = jnp.zeros((rank, rhs), jnp.float32)
        for slot in range(0, count, 4):
            matrix = jnp.concatenate([blocks(slot + k) for k in range(4)], axis=1)
            taken = [store[pick(slot + k)] for k in range(4)]
            picked = jnp.concatenate(
                [jnp.where(low, taken[0], taken[1]), jnp.where(low, taken[2], taken[3])], axis=1
            )
            field = field + dot(matrix, picked, ROWS_BY_ROWS)
        return field

    def one_group(group, carry):
        local1[group] = couple(
            lambda s: coarse_coupling_ref[group, s],
            coarse,
            lambda s: table_ref[at_coarse + group, s],
            far1,
        ).astype(jnp.bfloat16)
        return carry

    lax.fori_loop(0, groups, one_group, 0, unroll=2)

    def end_list(window, carry):
        @pl.when(in_window(window))
        def _():
            list_copy(window, window).wait_recv()
            list_copy(window, 2 * WINDOW - window).wait_send()

        return carry

    lax.fori_loop(0, WINDOWS, end_list, 0)

    def open_list(window, carry):
        for slot in range(half_slots):
            first, second = opened(listed_packed[window, slot])
            index = window * capacity + slot
            listed[index] = first
            listed[index + half_slots] = second
        return carry

    lax.fori_loop(0, WINDOWS, open_list, 0)

    for group in range(groups):
        coupling_load(group).wait()

    def one_leaf(leaf, carry):
        local0 = couple(
            lambda s: coupling_ref[leaf, s],
            listed,
            lambda s: table_ref[at_relay + leaf, s],
            far0,
        )
        downward = dot(transfer_ref[leaf], local1[leaf // CHILDREN], PLAIN)
        field = (local0 + downward).T.astype(jnp.bfloat16)
        span = pl.ds(pl.multiple_of(leaf * leaf_size, leaf_size), leaf_size)
        out_ref[:, span] = out_ref[:, span] + dot(field, basis_ref[leaf], PLAIN)
        return carry

    lax.fori_loop(0, leaf_count, one_leaf, 0, unroll=2)


def whole(sizes, spans, table, densities, points, weights, leaf_basis, transfer, coarse_coupling, coupling):
    rhs, columns = densities.shape
    leaf_count, rank, leaf_size = leaf_basis.shape
    total = sizes[0] * sizes[1]
    groups = leaf_count // CHILDREN
    capacity = spans[2]
    anywhere = pl.BlockSpec(memory_space=pl.ANY)
    rim = REACH * leaf_size
    dma = pltpu.SemaphoreType.DMA
    operands = (densities, points, weights, leaf_basis, transfer, coarse_coupling, coupling)
    held = [pltpu.VMEM(x.shape, x.dtype) for x in operands]
    half = jnp.bfloat16
    return pl.pallas_call(
        functools.partial(whole_kernel, sizes, spans),
        out_shape=jax.ShapeDtypeStruct((rhs, columns), jnp.float32),
        in_specs=[pl.BlockSpec(memory_space=pltpu.SMEM)] + [anywhere] * len(operands),
        out_specs=pl.BlockSpec(memory_space=pltpu.VMEM),
        scratch_shapes=held
        + [
            pltpu.VMEM((leaf_count, leaf_size, 48), half),
            pltpu.VMEM((leaf_count + 2 * REACH, 48, leaf_size), half),
            pltpu.VMEM((leaf_count + 2 * REACH, rhs, leaf_size), half),
            pltpu.VMEM((leaf_count, rhs, 2 * rank), half),
            pltpu.VMEM((WINDOWS, capacity // 2, rhs, 2 * rank), half),
            pltpu.VMEM((WINDOWS, capacity // 2, rhs, 2 * rank), half),
            pltpu.VMEM((total, groups // 2, rhs, 2 * rank), half),
            pltpu.VMEM((WINDOWS * capacity, rhs, 2 * rank), half),
            pltpu.VMEM((total * groups, rhs, 2 * rank), half),
            pltpu.VMEM((groups, rank, rhs), half),
            pltpu.VMEM((2, rhs, rim), half),
            pltpu.VMEM((2, 3, rim), jnp.float32),
            pltpu.VMEM((2, REACH, leaf_size), jnp.float32),
            dma((6,)),
            dma((groups,)),
            dma((2, 3)),
            dma((2, 3)),
            dma((WINDOWS,)),
            dma((WINDOWS,)),
            dma((total,)),
            dma((total,)),
        ],
        compiler_params=pltpu.CompilerParams(
            collective_id=0, has_side_effects=True, vmem_limit_bytes=63 * 1024 * 1024
        ),
        name="whole",
    )(table, *operands)


def local(
    sizes,
    densities,
    points,
    weights,
    near_offsets,
    leaf_basis,
    transfer,
    send_lists,
    relay_refs,
    leaf_coupling,
    coarse_refs,
    coarse_coupling,
):
    leaf_count, _, leaf_size = leaf_basis.shape
    lines = weights.reshape(leaf_count, leaf_size)
    tables = [near_offsets.T, send_lists[0].T, relay_refs, coarse_refs]
    width = max(array.shape[1] for array in tables)
    table = jnp.concatenate(
        [jnp.pad(array, ((0, 0), (0, width - array.shape[1]))) for array in tables], axis=0
    )
    spans = (
        near_offsets.shape[1],
        relay_refs.shape[1],
        send_lists.shape[2],
        coarse_refs.shape[1],
    )
    return whole(
        sizes,
        spans,
        table,
        densities,
        points,
        lines,
        leaf_basis,
        transfer,
        coarse_coupling,
        leaf_coupling,
    )


def solution(mesh):
    sizes = (mesh.shape["gx"], mesh.shape["gy"])
    in_specs = (
        P(None, ("gx", "gy")),
        P(None, ("gx", "gy")),
        P(("gx", "gy")),
        P(("gx", "gy"), None),
        P(("gx", "gy"), None, None),
        P(("gx", "gy"), None, None),
        P(("gx", "gy"), None, None),
        P(("gx", "gy"), None),
        P(("gx", "gy"), None, None, None),
        P(("gx", "gy"), None),
        P(("gx", "gy"), None, None, None),
    )
    out_specs = P(None, ("gx", "gy"))
    return jax.shard_map(
        functools.partial(local, sizes),
        mesh=mesh,
        in_specs=in_specs,
        out_specs=out_specs,
        check_vma=False,
    )
```

```python
import functools
import math

import jax
import jax.numpy as jnp
from jax import lax
from jax.experimental import pallas as pl
from jax.experimental.pallas import tpu as pltpu
from jax.sharding import PartitionSpec as P

REACH = 8
WINDOW = 8
CHILDREN = 8
WINDOWS = 2 * WINDOW + 1

core_square = 0.0004
four_pi = 4.0 * math.pi

MESH = pl.DeviceIdType.MESH
ROWS_BY_ROWS = (((1,), (1,)), ((), ()))
PLAIN = (((1,), (0,)), ((), ()))


def dot(left, right, dims):
    return lax.dot_general(left, right, dims, preferred_element_type=jnp.float32)


def split(values):
    first = values.astype(jnp.bfloat16).astype(jnp.float32)
    rest = values - first
    second = rest.astype(jnp.bfloat16).astype(jnp.float32)
    return first, second, rest - second


def features(points, weights):
    row = lax.broadcasted_iota(jnp.int32, (8, points.shape[1]), 0)
    x, y, z = (points[k : k + 1] - 0.5 for k in range(3))
    norm = x * x + y * y + z * z
    root = four_pi / weights
    scale = root * root
    shifted = jnp.where(row == 0, x, jnp.where(row == 1, y, z))
    left = jnp.where(row < 3, shifted, jnp.where(row == 3, norm, jnp.where(row == 4, 1.0, 0.0)))
    right = scale * jnp.where(
        row < 3,
        -2.0 * shifted,
        jnp.where(row == 3, 1.0, jnp.where(row == 4, norm + core_square, 0.0)),
    )
    a1, a2, a3 = split(left)
    b1, b2, b3 = split(right)
    return (
        jnp.concatenate([a1, a1, a2, a1, a3, a2], axis=0),
        jnp.concatenate([b1, b2, b1, b3, b1, b2], axis=0),
    )


def whole_kernel(
    sizes,
    offsets_any,
    lists_any,
    relay_any,
    refs_any,
    dens_any,
    points_any,
    weights_any,
    basis_any,
    transfer_any,
    coarse_coupling_any,
    coupling_any,
    out_ref,
    offsets_ref,
    lists_ref,
    relay_ref,
    refs_ref,
    dens_ref,
    points_ref,
    weights_ref,
    basis_ref,
    transfer_ref,
    coarse_coupling_ref,
    coupling_ref,
    row_feat,
    col_feat,
    values,
    coeff,
    outgoing,
    listed_packed,
    coarse_packed,
    listed,
    coarse,
    local1,
    halo_dens,
    halo_points,
    halo_weights,
    load_sems,
    coupling_sems,
    halo_send,
    halo_recv,
    list_send,
    list_recv,
    inner_send,
    inner_recv,
    outer_send,
    outer_recv,
):
    n_gx, n_gy = sizes
    total = n_gx * n_gy
    me = lax.axis_index("gx") * n_gy + lax.axis_index("gy")
    leaf_count, rank, leaf_size = basis_ref.shape
    rhs = dens_ref.shape[0]
    slots, capacity = offsets_ref.shape[0], lists_ref.shape[0]
    far0, far1 = relay_ref.shape[1], refs_ref.shape[1]
    groups = leaf_count // CHILDREN
    half_slots = capacity // 2
    rim = REACH * leaf_size
    columns = leaf_count * leaf_size

    loads = [
        pltpu.make_async_copy(source, target, load_sems.at[k])
        for k, (source, target) in enumerate(
            [
                (lists_any, lists_ref),
                (dens_any, dens_ref),
                (basis_any, basis_ref),
                (transfer_any, transfer_ref),
                (points_any, points_ref),
                (weights_any, weights_ref),
                (offsets_any, offsets_ref),
                (refs_any, refs_ref),
                (relay_any, relay_ref),
                (coarse_coupling_any, coarse_coupling_ref),
            ]
        )
    ]
    for load in loads:
        load.start()

    def coupling_load(group):
        span = pl.ds(group * CHILDREN, CHILDREN)
        return pltpu.make_async_copy(
            coupling_any.at[span], coupling_ref.at[span], coupling_sems.at[group]
        )

    for group in range(groups):
        coupling_load(group).start()

    def place(index):
        return (index // n_gy, index % n_gy)

    barrier = pltpu.get_barrier_semaphore()

    def greet(step, carry):
        other = (me + step) % total
        pl.semaphore_signal(barrier, inc=1, device_id=place(other), device_id_type=MESH)
        return carry

    lax.fori_loop(1, total, greet, 0)
    for load in loads[:4]:
        load.wait()

    low = lax.broadcasted_iota(jnp.int32, (rhs, 2 * rank), 1) < rank

    def upward(pair, carry):
        parents = []
        for g in range(2):
            parent = None
            for child in range(CHILDREN):
                leaf = (pair * 2 + g) * CHILDREN + child
                start = pl.multiple_of(leaf * leaf_size, leaf_size)
                basis = basis_ref[leaf]
                doubled = jnp.concatenate([basis, basis], axis=0)
                both = dot(dens_ref[:, pl.ds(start, leaf_size)], doubled, ROWS_BY_ROWS)
                both = both.astype(jnp.bfloat16)
                coeff[leaf] = both
                term = dot(both[:, :rank], transfer_ref[leaf], PLAIN)
                parent = term if parent is None else parent + term
            parents.append(parent)
        coarse_packed[me, pair] = jnp.concatenate(parents, axis=1).astype(jnp.bfloat16)
        return carry

    lax.fori_loop(0, groups // 2, upward, 0)

    def gather(window, carry):
        for slot in range(half_slots):
            first = coeff[lists_ref[slot, window]]
            second = coeff[lists_ref[slot + half_slots, window]]
            outgoing[window, slot] = jnp.where(low, first, second)
        return carry

    lax.fori_loop(0, WINDOWS, gather, 0)
    listed_packed[WINDOW] = outgoing[WINDOW]
    for load in loads[4:9]:
        load.wait()

    pl.semaphore_wait(barrier, total - 1)

    def halo(side):
        other = place(me - 1 if side == 0 else me + 1)
        start = 0 if side == 0 else columns - rim
        leaf = 0 if side == 0 else leaf_count - REACH
        parts = [
            (dens_ref.at[:, pl.ds(start, rim)], halo_dens),
            (points_ref.at[:, pl.ds(start, rim)], halo_points),
            (weights_ref.at[pl.ds(leaf, REACH)], halo_weights),
        ]
        return [
            pltpu.make_async_remote_copy(
                src_ref=source,
                dst_ref=target.at[1 - side],
                send_sem=halo_send.at[side, kind],
                recv_sem=halo_recv.at[1 - side, kind],
                device_id=other,
                device_id_type=MESH,
            )
            for kind, (source, target) in enumerate(parts)
        ]

    @pl.when(me > 0)
    def _():
        for copy in halo(0):
            copy.start()

    @pl.when(me < total - 1)
    def _():
        for copy in halo(1):
            copy.start()

    my_gx, my_gy = lax.axis_index("gx"), lax.axis_index("gy")

    def inner_copy(other, slot):
        block = coarse_packed.at[my_gx * n_gy + slot]
        return pltpu.make_async_remote_copy(
            src_ref=block,
            dst_ref=block,
            send_sem=inner_send.at[other],
            recv_sem=inner_recv.at[slot],
            device_id=(my_gx, other),
            device_id_type=MESH,
        )

    def outer_copy(other, slot):
        block = coarse_packed.at[pl.ds(slot * n_gy, n_gy)]
        return pltpu.make_async_remote_copy(
            src_ref=block,
            dst_ref=block,
            send_sem=outer_send.at[other],
            recv_sem=outer_recv.at[slot],
            device_id=(other, my_gy),
            device_id_type=MESH,
        )

    def list_copy(window, landing):
        return pltpu.make_async_remote_copy(
            src_ref=outgoing.at[window],
            dst_ref=listed_packed.at[landing],
            send_sem=list_send.at[window],
            recv_sem=list_recv.at[landing],
            device_id=place(me + window - WINDOW),
            device_id_type=MESH,
        )

    def in_window(window):
        other = me + window - WINDOW
        return (window != WINDOW) & (other >= 0) & (other < total)

    def send_list(window, carry):
        @pl.when(in_window(window))
        def _():
            list_copy(window, 2 * WINDOW - window).start()

        return carry

    def send_inner(step, carry):
        inner_copy((my_gy + step) % n_gy, my_gy).start()
        return carry

    lax.fori_loop(1, n_gy, send_inner, 0)
    lax.fori_loop(0, WINDOWS, send_list, 0)

    batch = 4

    def prepare(first_leaf, points, weights, dens, own):
        line = jnp.concatenate([weights[k : k + 1] for k in range(batch)], axis=1)
        left, right = features(points, line)
        right = right.astype(jnp.bfloat16)
        for k in range(batch):
            part = slice(k * leaf_size, (k + 1) * leaf_size)
            col_feat[first_leaf + k] = right[:, part]
            values[first_leaf + k] = dens[:, part]
            if own:
                row_feat[first_leaf - REACH + k] = left[:, part].T.astype(jnp.bfloat16)

    def prepare_own(step, carry):
        span = pl.ds(pl.multiple_of(step * batch * leaf_size, batch * leaf_size), batch * leaf_size)
        lines = weights_ref[pl.ds(step * batch, batch)]
        prepare(REACH + step * batch, points_ref[:, span], lines, dens_ref[:, span], True)
        return carry

    lax.fori_loop(0, leaf_count // batch, prepare_own, 0)

    def near_leaf(leaf, carry):
        mine = row_feat[leaf]
        field = jnp.zeros((leaf_size, rhs), jnp.float32)
        partners = [leaf + REACH + offsets_ref[slot, leaf] for slot in range(slots)]
        for first in range(0, slots, 2):
            some = partners[first : first + 2]
            cols = jnp.concatenate([col_feat[p] for p in some], axis=1)
            vals = jnp.concatenate([values[p] for p in some], axis=1)
            kernel = lax.rsqrt(dot(mine, cols, PLAIN)).astype(jnp.bfloat16)
            field = field + dot(kernel, vals, ROWS_BY_ROWS)
        out_ref[:, pl.ds(pl.multiple_of(leaf * leaf_size, leaf_size), leaf_size)] = field.T
        return carry

    middle = leaf_count // 2
    lax.fori_loop(REACH, middle, near_leaf, 0, unroll=2)

    def end_inner(step, carry):
        other = (my_gy + step) % n_gy
        inner_copy(other, other).wait_recv()
        inner_copy(other, my_gy).wait_send()
        return carry

    lax.fori_loop(1, n_gy, end_inner, 0)

    def send_outer(step, carry):
        outer_copy((my_gx + step) % n_gx, my_gx).start()
        return carry

    lax.fori_loop(1, n_gx, send_outer, 0)
    lax.fori_loop(middle, leaf_count - REACH, near_leaf, 0, unroll=2)

    @pl.when(me == 0)
    def _():
        halo_dens[0] = jnp.zeros(halo_dens.shape[1:], halo_dens.dtype)
        halo_points[0] = jnp.zeros(halo_points.shape[1:], halo_points.dtype)
        halo_weights[0] = jnp.ones(halo_weights.shape[1:], halo_weights.dtype)

    @pl.when(me == total - 1)
    def _():
        halo_dens[1] = jnp.zeros(halo_dens.shape[1:], halo_dens.dtype)
        halo_points[1] = jnp.zeros(halo_points.shape[1:], halo_points.dtype)
        halo_weights[1] = jnp.ones(halo_weights.shape[1:], halo_weights.dtype)

    @pl.when(me > 0)
    def _():
        for copy in halo(1):
            copy.wait_recv()
        for copy in halo(0):
            copy.wait_send()

    @pl.when(me < total - 1)
    def _():
        for copy in halo(0):
            copy.wait_recv()
        for copy in halo(1):
            copy.wait_send()

    for side in range(2):
        base = 0 if side == 0 else REACH + leaf_count

        def prepare_rim(step, carry, side=side, base=base):
            width = batch * leaf_size
            span = pl.ds(pl.multiple_of(step * width, width), width)
            lines = halo_weights[side, pl.ds(step * batch, batch)]
            dens = halo_dens[side, :, span]
            prepare(base + step * batch, halo_points[side, :, span], lines, dens, False)
            return carry

        lax.fori_loop(0, REACH // batch, prepare_rim, 0)

    lax.fori_loop(0, REACH, near_leaf, 0, unroll=2)
    lax.fori_loop(leaf_count - REACH, leaf_count, near_leaf, 0, unroll=2)

    def end_outer(step, carry):
        other = (my_gx + step) % n_gx
        outer_copy(other, other).wait_recv()
        outer_copy(other, my_gx).wait_send()
        return carry

    lax.fori_loop(1, n_gx, end_outer, 0)

    def opened(packed):
        both = packed.astype(jnp.float32)
        turned = pltpu.roll(both, rank, 1)
        return (
            jnp.where(low, both, turned).astype(jnp.bfloat16),
            jnp.where(low, turned, both).astype(jnp.bfloat16),
        )

    pairs = groups // 2

    def open_coarse(step, carry):
        for k in range(4 * pairs):
            first, second = opened(coarse_packed[step * 4 + k // pairs, k % pairs])
            index = step * 8 * pairs + 2 * k
            coarse[index] = first
            coarse[index + 1] = second
        return carry

    lax.fori_loop(0, total // 4, open_coarse, 0)
    loads[9].wait()

    def couple(blocks, store, pick, count):
        field = jnp.zeros((rank, rhs), jnp.float32)
        for slot in range(0, count, 4):
            matrix = jnp.concatenate([blocks(slot + k) for k in range(4)], axis=1)
            taken = [store[pick(slot + k)] for k in range(4)]
            picked = jnp.concatenate(
                [jnp.where(low, taken[0], taken[1]), jnp.where(low, taken[2], taken[3])], axis=1
            )
            field = field + dot(matrix, picked, ROWS_BY_ROWS)
        return field

    def one_group(group, carry):
        local1[group] = couple(
            lambda s: coarse_coupling_ref[group, s],
            coarse,
            lambda s: refs_ref[group, s],
            far1,
        ).astype(jnp.bfloat16)
        return carry

    lax.fori_loop(0, groups, one_group, 0, unroll=2)

    def end_list(window, carry):
        @pl.when(in_window(window))
        def _():
            list_copy(window, window).wait_recv()
            list_copy(window, 2 * WINDOW - window).wait_send()

        return carry

    lax.fori_loop(0, WINDOWS, end_list, 0)

    def open_list(window, carry):
        for slot in range(half_slots):
            first, second = opened(listed_packed[window, slot])
            index = window * capacity + slot
            listed[index] = first
            listed[index + half_slots] = second
        return carry

    lax.fori_loop(0, WINDOWS, open_list, 0)

    for group in range(groups):
        coupling_load(group).wait()

    def one_leaf(leaf, carry):
        local0 = couple(
            lambda s: coupling_ref[leaf, s],
            listed,
            lambda s: relay_ref[leaf, s],
            far0,
        )
        downward = dot(transfer_ref[leaf], local1[leaf // CHILDREN], PLAIN)
        field = (local0 + downward).T.astype(jnp.bfloat16)
        span = pl.ds(pl.multiple_of(leaf * leaf_size, leaf_size), leaf_size)
        out_ref[:, span] = out_ref[:, span] + dot(field, basis_ref[leaf], PLAIN)
        return carry

    lax.fori_loop(0, leaf_count, one_leaf, 0, unroll=2)


def whole(sizes, tables, densities, points, weights, leaf_basis, transfer, coarse_coupling, coupling):
    rhs, columns = densities.shape
    leaf_count, rank, leaf_size = leaf_basis.shape
    total = sizes[0] * sizes[1]
    groups = leaf_count // CHILDREN
    capacity = tables[1].shape[0]
    anywhere = pl.BlockSpec(memory_space=pl.ANY)
    rim = REACH * leaf_size
    dma = pltpu.SemaphoreType.DMA
    operands = (densities, points, weights, leaf_basis, transfer, coarse_coupling, coupling)
    held = [pltpu.SMEM(x.shape, x.dtype) for x in tables]
    held += [pltpu.VMEM(x.shape, x.dtype) for x in operands]
    half = jnp.bfloat16
    return pl.pallas_call(
        functools.partial(whole_kernel, sizes),
        out_shape=jax.ShapeDtypeStruct((rhs, columns), jnp.float32),
        in_specs=[anywhere] * (len(tables) + len(operands)),
        out_specs=pl.BlockSpec(memory_space=pltpu.VMEM),
        scratch_shapes=held
        + [
            pltpu.VMEM((leaf_count, leaf_size, 48), half),
            pltpu.VMEM((leaf_count + 2 * REACH, 48, leaf_size), half),
            pltpu.VMEM((leaf_count + 2 * REACH, rhs, leaf_size), half),
            pltpu.VMEM((leaf_count, rhs, 2 * rank), half),
            pltpu.VMEM((WINDOWS, capacity // 2, rhs, 2 * rank), half),
            pltpu.VMEM((WINDOWS, capacity // 2, rhs, 2 * rank), half),
            pltpu.VMEM((total, groups // 2, rhs, 2 * rank), half),
            pltpu.VMEM((WINDOWS * capacity, rhs, 2 * rank), half),
            pltpu.VMEM((total * groups, rhs, 2 * rank), half),
            pltpu.VMEM((groups, rank, rhs), half),
            pltpu.VMEM((2, rhs, rim), half),
            pltpu.VMEM((2, 3, rim), jnp.float32),
            pltpu.VMEM((2, REACH, leaf_size), jnp.float32),
            dma((10,)),
            dma((groups,)),
            dma((2, 3)),
            dma((2, 3)),
            dma((WINDOWS,)),
            dma((WINDOWS,)),
            dma((sizes[1],)),
            dma((sizes[1],)),
            dma((sizes[0],)),
            dma((sizes[0],)),
        ],
        compiler_params=pltpu.CompilerParams(
            collective_id=0, has_side_effects=True, vmem_limit_bytes=63 * 1024 * 1024
        ),
        name="whole",
    )(*tables, *operands)


def local(
    sizes,
    densities,
    points,
    weights,
    near_offsets,
    leaf_basis,
    transfer,
    send_lists,
    relay_refs,
    leaf_coupling,
    coarse_refs,
    coarse_coupling,
):
    leaf_count, _, leaf_size = leaf_basis.shape
    lines = weights.reshape(leaf_count, leaf_size)
    tables = (near_offsets.T, send_lists[0].T, relay_refs, coarse_refs)
    return whole(
        sizes,
        tables,
        densities,
        points,
        lines,
        leaf_basis,
        transfer,
        coarse_coupling,
        leaf_coupling,
    )


def solution(mesh):
    sizes = (mesh.shape["gx"], mesh.shape["gy"])
    in_specs = (
        P(None, ("gx", "gy")),
        P(None, ("gx", "gy")),
        P(("gx", "gy")),
        P(("gx", "gy"), None),
        P(("gx", "gy"), None, None),
        P(("gx", "gy"), None, None),
        P(("gx", "gy"), None, None),
        P(("gx", "gy"), None),
        P(("gx", "gy"), None, None, None),
        P(("gx", "gy"), None),
        P(("gx", "gy"), None, None, None),
    )
    out_specs = P(None, ("gx", "gy"))
    return jax.shard_map(
        functools.partial(local, sizes),
        mesh=mesh,
        in_specs=in_specs,
        out_specs=out_specs,
        check_vma=False,
    )
```

```python
import functools
import math

import jax
import jax.numpy as jnp
from jax import lax
from jax.experimental import pallas as pl
from jax.experimental.pallas import tpu as pltpu
from jax.sharding import PartitionSpec as P

REACH = 8
WINDOW = 8
CHILDREN = 8
WINDOWS = 2 * WINDOW + 1

core_square = 0.0004
four_pi = 4.0 * math.pi

MESH = pl.DeviceIdType.MESH
ROWS_BY_ROWS = (((1,), (1,)), ((), ()))
PLAIN = (((1,), (0,)), ((), ()))


def dot(left, right, dims):
    return lax.dot_general(left, right, dims, preferred_element_type=jnp.float32)


def split(values):
    first = values.astype(jnp.bfloat16).astype(jnp.float32)
    rest = values - first
    second = rest.astype(jnp.bfloat16).astype(jnp.float32)
    return first, second, rest - second


def features(points, weights):
    row = lax.broadcasted_iota(jnp.int32, (8, points.shape[1]), 0)
    x, y, z = (points[k : k + 1] - 0.5 for k in range(3))
    norm = x * x + y * y + z * z
    root = four_pi / weights
    scale = root * root
    shifted = jnp.where(row == 0, x, jnp.where(row == 1, y, z))
    left = jnp.where(row < 3, shifted, jnp.where(row == 3, norm, jnp.where(row == 4, 1.0, 0.0)))
    right = scale * jnp.where(
        row < 3,
        -2.0 * shifted,
        jnp.where(row == 3, 1.0, jnp.where(row == 4, norm + core_square, 0.0)),
    )
    a1, a2, a3 = split(left)
    b1, b2, b3 = split(right)
    return (
        jnp.concatenate([a1, a1, a2, a1, a3, a2], axis=0),
        jnp.concatenate([b1, b2, b1, b3, b1, b2], axis=0),
    )


def whole_kernel(
    sizes,
    offsets_any,
    lists_any,
    relay_any,
    refs_any,
    dens_any,
    points_any,
    weights_any,
    basis_any,
    transfer_any,
    coarse_coupling_any,
    coupling_any,
    out_ref,
    offsets_ref,
    lists_ref,
    relay_ref,
    refs_ref,
    dens_ref,
    points_ref,
    weights_ref,
    basis_ref,
    transfer_ref,
    coarse_coupling_ref,
    coupling_ref,
    row_feat,
    col_feat,
    values,
    coeff,
    outgoing,
    listed_packed,
    coarse_packed,
    listed,
    coarse,
    local1,
    halo_dens,
    halo_points,
    halo_weights,
    load_sems,
    coupling_sems,
    halo_send,
    halo_recv,
    list_send,
    list_recv,
    inner_send,
    inner_recv,
    outer_send,
    outer_recv,
):
    n_gx, n_gy = sizes
    total = n_gx * n_gy
    me = lax.axis_index("gx") * n_gy + lax.axis_index("gy")
    leaf_count, rank, leaf_size = basis_ref.shape
    rhs = dens_ref.shape[0]
    slots, capacity = offsets_ref.shape[0], lists_ref.shape[0]
    far0, far1 = relay_ref.shape[1], refs_ref.shape[1]
    groups = leaf_count // CHILDREN
    half_slots = capacity // 2
    rim = REACH * leaf_size
    columns = leaf_count * leaf_size

    loads = [
        pltpu.make_async_copy(source, target, load_sems.at[k])
        for k, (source, target) in enumerate(
            [
                (lists_any, lists_ref),
                (dens_any, dens_ref),
                (basis_any, basis_ref),
                (transfer_any, transfer_ref),
                (points_any, points_ref),
                (weights_any, weights_ref),
                (offsets_any, offsets_ref),
                (refs_any, refs_ref),
                (relay_any, relay_ref),
                (coarse_coupling_any, coarse_coupling_ref),
            ]
        )
    ]
    for load in loads:
        load.start()

    def coupling_load(group):
        span = pl.ds(group * CHILDREN, CHILDREN)
        return pltpu.make_async_copy(
            coupling_any.at[span], coupling_ref.at[span], coupling_sems.at[group]
        )

    for group in range(groups):
        coupling_load(group).start()

    def place(index):
        return (index // n_gy, index % n_gy)

    barrier = pltpu.get_barrier_semaphore()

    def greet(step, carry):
        other = (me + step) % total
        pl.semaphore_signal(barrier, inc=1, device_id=place(other), device_id_type=MESH)
        return carry

    lax.fori_loop(1, total, greet, 0)
    for load in loads[:4]:
        load.wait()

    low = lax.broadcasted_iota(jnp.int32, (rhs, 2 * rank), 1) < rank

    def upward(pair, carry):
        parents = []
        for g in range(2):
            parent = None
            for child in range(CHILDREN):
                leaf = (pair * 2 + g) * CHILDREN + child
                start = pl.multiple_of(leaf * leaf_size, leaf_size)
                basis = basis_ref[leaf]
                doubled = jnp.concatenate([basis, basis], axis=0)
                both = dot(dens_ref[:, pl.ds(start, leaf_size)], doubled, ROWS_BY_ROWS)
                both = both.astype(jnp.bfloat16)
                coeff[leaf] = both
                term = dot(both[:, :rank], transfer_ref[leaf], PLAIN)
                parent = term if parent is None else parent + term
            parents.append(parent)
        coarse_packed[me, pair] = jnp.concatenate(parents, axis=1).astype(jnp.bfloat16)
        return carry

    lax.fori_loop(0, groups // 2, upward, 0)

    def gather(window, carry):
        for slot in range(half_slots):
            first = coeff[lists_ref[slot, window]]
            second = coeff[lists_ref[slot + half_slots, window]]
            outgoing[window, slot] = jnp.where(low, first, second)
        return carry

    lax.fori_loop(0, WINDOWS, gather, 0)
    listed_packed[WINDOW] = outgoing[WINDOW]
    for load in loads[4:9]:
        load.wait()

    pl.semaphore_wait(barrier, total - 1)

    def halo(side):
        other = place(me - 1 if side == 0 else me + 1)
        start = 0 if side == 0 else columns - rim
        leaf = 0 if side == 0 else leaf_count - REACH
        parts = [
            (dens_ref.at[:, pl.ds(start, rim)], halo_dens),
            (points_ref.at[:, pl.ds(start, rim)], halo_points),
            (weights_ref.at[pl.ds(leaf, REACH)], halo_weights),
        ]
        return [
            pltpu.make_async_remote_copy(
                src_ref=source,
                dst_ref=target.at[1 - side],
                send_sem=halo_send.at[side, kind],
                recv_sem=halo_recv.at[1 - side, kind],
                device_id=other,
                device_id_type=MESH,
            )
            for kind, (source, target) in enumerate(parts)
        ]

    @pl.when(me > 0)
    def _():
        for copy in halo(0):
            copy.start()

    @pl.when(me < total - 1)
    def _():
        for copy in halo(1):
            copy.start()

    my_gx, my_gy = lax.axis_index("gx"), lax.axis_index("gy")

    def inner_copy(other, slot):
        block = coarse_packed.at[my_gx * n_gy + slot]
        return pltpu.make_async_remote_copy(
            src_ref=block,
            dst_ref=block,
            send_sem=inner_send.at[other],
            recv_sem=inner_recv.at[slot],
            device_id=(my_gx, other),
            device_id_type=MESH,
        )

    def outer_copy(other, slot):
        block = coarse_packed.at[pl.ds(slot * n_gy, n_gy)]
        return pltpu.make_async_remote_copy(
            src_ref=block,
            dst_ref=block,
            send_sem=outer_send.at[other],
            recv_sem=outer_recv.at[slot],
            device_id=(other, my_gy),
            device_id_type=MESH,
        )

    def list_copy(window, landing):
        return pltpu.make_async_remote_copy(
            src_ref=outgoing.at[window],
            dst_ref=listed_packed.at[landing],
            send_sem=list_send.at[window],
            recv_sem=list_recv.at[landing],
            device_id=place(me + window - WINDOW),
            device_id_type=MESH,
        )

    def in_window(window):
        other = me + window - WINDOW
        return (window != WINDOW) & (other >= 0) & (other < total)

    def send_list(window, carry):
        @pl.when(in_window(window))
        def _():
            list_copy(window, 2 * WINDOW - window).start()

        return carry

    def send_inner(step, carry):
        inner_copy((my_gy + step) % n_gy, my_gy).start()
        return carry

    lax.fori_loop(1, n_gy, send_inner, 0)
    lax.fori_loop(0, WINDOWS, send_list, 0)

    batch = 4

    def prepare(first_leaf, points, weights, dens, own):
        line = jnp.concatenate([weights[k : k + 1] for k in range(batch)], axis=1)
        left, right = features(points, line)
        right = right.astype(jnp.bfloat16)
        for k in range(batch):
            part = slice(k * leaf_size, (k + 1) * leaf_size)
            col_feat[first_leaf + k] = right[:, part]
            values[first_leaf + k] = dens[:, part]
            if own:
                row_feat[first_leaf - REACH + k] = left[:, part].T.astype(jnp.bfloat16)

    def prepare_own(step, carry):
        span = pl.ds(pl.multiple_of(step * batch * leaf_size, batch * leaf_size), batch * leaf_size)
        lines = weights_ref[pl.ds(step * batch, batch)]
        prepare(REACH + step * batch, points_ref[:, span], lines, dens_ref[:, span], True)
        return carry

    lax.fori_loop(0, leaf_count // batch, prepare_own, 0)

    def near_leaf(leaf, carry):
        mine = row_feat[leaf]
        partners = [leaf + REACH + offsets_ref[slot, leaf] for slot in range(slots)]
        kernels = []
        for first in range(0, slots, 2):
            some = partners[first : first + 2]
            cols = jnp.concatenate([col_feat[p] for p in some], axis=1)
            kernels.append(lax.rsqrt(dot(mine, cols, PLAIN).astype(jnp.bfloat16)))
        vals = jnp.concatenate([values[p] for p in partners], axis=1)
        field = dot(jnp.concatenate(kernels, axis=1), vals, ROWS_BY_ROWS)
        out_ref[:, pl.ds(pl.multiple_of(leaf * leaf_size, leaf_size), leaf_size)] = field.T
        return carry

    middle = leaf_count // 2
    lax.fori_loop(REACH, middle, near_leaf, 0, unroll=2)

    def end_inner(step, carry):
        other = (my_gy + step) % n_gy
        inner_copy(other, other).wait_recv()
        inner_copy(other, my_gy).wait_send()
        return carry

    lax.fori_loop(1, n_gy, end_inner, 0)

    def send_outer(step, carry):
        outer_copy((my_gx + step) % n_gx, my_gx).start()
        return carry

    lax.fori_loop(1, n_gx, send_outer, 0)
    lax.fori_loop(middle, leaf_count - REACH, near_leaf, 0, unroll=2)

    @pl.when(me == 0)
    def _():
        halo_dens[0] = jnp.zeros(halo_dens.shape[1:], halo_dens.dtype)
        halo_points[0] = jnp.zeros(halo_points.shape[1:], halo_points.dtype)
        halo_weights[0] = jnp.ones(halo_weights.shape[1:], halo_weights.dtype)

    @pl.when(me == total - 1)
    def _():
        halo_dens[1] = jnp.zeros(halo_dens.shape[1:], halo_dens.dtype)
        halo_points[1] = jnp.zeros(halo_points.shape[1:], halo_points.dtype)
        halo_weights[1] = jnp.ones(halo_weights.shape[1:], halo_weights.dtype)

    @pl.when(me > 0)
    def _():
        for copy in halo(1):
            copy.wait_recv()
        for copy in halo(0):
            copy.wait_send()

    @pl.when(me < total - 1)
    def _():
        for copy in halo(0):
            copy.wait_recv()
        for copy in halo(1):
            copy.wait_send()

    for side in range(2):
        base = 0 if side == 0 else REACH + leaf_count

        def prepare_rim(step, carry, side=side, base=base):
            width = batch * leaf_size
            span = pl.ds(pl.multiple_of(step * width, width), width)
            lines = halo_weights[side, pl.ds(step * batch, batch)]
            dens = halo_dens[side, :, span]
            prepare(base + step * batch, halo_points[side, :, span], lines, dens, False)
            return carry

        lax.fori_loop(0, REACH // batch, prepare_rim, 0)

    lax.fori_loop(0, REACH, near_leaf, 0, unroll=2)
    lax.fori_loop(leaf_count - REACH, leaf_count, near_leaf, 0, unroll=2)

    def end_outer(step, carry):
        other = (my_gx + step) % n_gx
        outer_copy(other, other).wait_recv()
        outer_copy(other, my_gx).wait_send()
        return carry

    lax.fori_loop(1, n_gx, end_outer, 0)

    def opened(packed):
        both = packed.astype(jnp.float32)
        turned = pltpu.roll(both, rank, 1)
        return (
            jnp.where(low, both, turned).astype(jnp.bfloat16),
            jnp.where(low, turned, both).astype(jnp.bfloat16),
        )

    pairs = groups // 2

    def open_coarse(step, carry):
        for k in range(4 * pairs):
            first, second = opened(coarse_packed[step * 4 + k // pairs, k % pairs])
            index = step * 8 * pairs + 2 * k
            coarse[index] = first
            coarse[index + 1] = second
        return carry

    lax.fori_loop(0, total // 4, open_coarse, 0)
    loads[9].wait()

    def couple(blocks, store, pick, count):
        matrix = jnp.concatenate([blocks(slot) for slot in range(count)], axis=1)
        taken = [store[pick(slot)] for slot in range(count)]
        picked = [jnp.where(low, taken[k], taken[k + 1]) for k in range(0, count, 2)]
        return dot(matrix, jnp.concatenate(picked, axis=1), ROWS_BY_ROWS)

    def one_group(group, carry):
        local1[group] = couple(
            lambda s: coarse_coupling_ref[group, s],
            coarse,
            lambda s: refs_ref[group, s],
            far1,
        ).astype(jnp.bfloat16)
        return carry

    lax.fori_loop(0, groups, one_group, 0, unroll=2)

    def end_list(window, carry):
        @pl.when(in_window(window))
        def _():
            list_copy(window, window).wait_recv()
            list_copy(window, 2 * WINDOW - window).wait_send()

        return carry

    lax.fori_loop(0, WINDOWS, end_list, 0)

    def open_list(window, carry):
        for slot in range(half_slots):
            first, second = opened(listed_packed[window, slot])
            index = window * capacity + slot
            listed[index] = first
            listed[index + half_slots] = second
        return carry

    lax.fori_loop(0, WINDOWS, open_list, 0)

    for group in range(groups):
        coupling_load(group).wait()

    def one_leaf(leaf, carry):
        local0 = couple(
            lambda s: coupling_ref[leaf, s],
            listed,
            lambda s: relay_ref[leaf, s],
            far0,
        )
        downward = dot(transfer_ref[leaf], local1[leaf // CHILDREN], PLAIN)
        field = (local0 + downward).T.astype(jnp.bfloat16)
        span = pl.ds(pl.multiple_of(leaf * leaf_size, leaf_size), leaf_size)
        out_ref[:, span] = out_ref[:, span] + dot(field, basis_ref[leaf], PLAIN)
        return carry

    lax.fori_loop(0, leaf_count, one_leaf, 0, unroll=2)


def whole(sizes, tables, densities, points, weights, leaf_basis, transfer, coarse_coupling, coupling):
    rhs, columns = densities.shape
    leaf_count, rank, leaf_size = leaf_basis.shape
    total = sizes[0] * sizes[1]
    groups = leaf_count // CHILDREN
    capacity = tables[1].shape[0]
    anywhere = pl.BlockSpec(memory_space=pl.ANY)
    rim = REACH * leaf_size
    dma = pltpu.SemaphoreType.DMA
    operands = (densities, points, weights, leaf_basis, transfer, coarse_coupling, coupling)
    held = [pltpu.SMEM(x.shape, x.dtype) for x in tables]
    held += [pltpu.VMEM(x.shape, x.dtype) for x in operands]
    half = jnp.bfloat16
    return pl.pallas_call(
        functools.partial(whole_kernel, sizes),
        out_shape=jax.ShapeDtypeStruct((rhs, columns), jnp.float32),
        in_specs=[anywhere] * (len(tables) + len(operands)),
        out_specs=pl.BlockSpec(memory_space=pltpu.VMEM),
        scratch_shapes=held
        + [
            pltpu.VMEM((leaf_count, leaf_size, 48), half),
            pltpu.VMEM((leaf_count + 2 * REACH, 48, leaf_size), half),
            pltpu.VMEM((leaf_count + 2 * REACH, rhs, leaf_size), half),
            pltpu.VMEM((leaf_count, rhs, 2 * rank), half),
            pltpu.VMEM((WINDOWS, capacity // 2, rhs, 2 * rank), half),
            pltpu.VMEM((WINDOWS, capacity // 2, rhs, 2 * rank), half),
            pltpu.VMEM((total, groups // 2, rhs, 2 * rank), half),
            pltpu.VMEM((WINDOWS * capacity, rhs, 2 * rank), half),
            pltpu.VMEM((total * groups, rhs, 2 * rank), half),
            pltpu.VMEM((groups, rank, rhs), half),
            pltpu.VMEM((2, rhs, rim), half),
            pltpu.VMEM((2, 3, rim), jnp.float32),
            pltpu.VMEM((2, REACH, leaf_size), jnp.float32),
            dma((10,)),
            dma((groups,)),
            dma((2, 3)),
            dma((2, 3)),
            dma((WINDOWS,)),
            dma((WINDOWS,)),
            dma((sizes[1],)),
            dma((sizes[1],)),
            dma((sizes[0],)),
            dma((sizes[0],)),
        ],
        compiler_params=pltpu.CompilerParams(
            collective_id=0, has_side_effects=True, vmem_limit_bytes=63 * 1024 * 1024
        ),
        name="whole",
    )(*tables, *operands)


def local(
    sizes,
    densities,
    points,
    weights,
    near_offsets,
    leaf_basis,
    transfer,
    send_lists,
    relay_refs,
    leaf_coupling,
    coarse_refs,
    coarse_coupling,
):
    leaf_count, _, leaf_size = leaf_basis.shape
    lines = weights.reshape(leaf_count, leaf_size)
    tables = (near_offsets.T, send_lists[0].T, relay_refs, coarse_refs)
    return whole(
        sizes,
        tables,
        densities,
        points,
        lines,
        leaf_basis,
        transfer,
        coarse_coupling,
        leaf_coupling,
    )


def solution(mesh):
    sizes = (mesh.shape["gx"], mesh.shape["gy"])
    in_specs = (
        P(None, ("gx", "gy")),
        P(None, ("gx", "gy")),
        P(("gx", "gy")),
        P(("gx", "gy"), None),
        P(("gx", "gy"), None, None),
        P(("gx", "gy"), None, None),
        P(("gx", "gy"), None, None),
        P(("gx", "gy"), None),
        P(("gx", "gy"), None, None, None),
        P(("gx", "gy"), None),
        P(("gx", "gy"), None, None, None),
    )
    out_specs = P(None, ("gx", "gy"))
    return jax.shard_map(
        functools.partial(local, sizes),
        mesh=mesh,
        in_specs=in_specs,
        out_specs=out_specs,
        check_vma=False,
    )
```

```python
import functools
import math

import jax
import jax.numpy as jnp
from jax import lax
from jax.experimental import pallas as pl
from jax.experimental.pallas import tpu as pltpu
from jax.sharding import PartitionSpec as P

REACH = 8
WINDOW = 8
CHILDREN = 8
WINDOWS = 2 * WINDOW + 1

core_square = 0.0004
four_pi = 4.0 * math.pi

MESH = pl.DeviceIdType.MESH
ROWS_BY_ROWS = (((1,), (1,)), ((), ()))
PLAIN = (((1,), (0,)), ((), ()))


def dot(left, right, dims):
    return lax.dot_general(left, right, dims, preferred_element_type=jnp.float32)


def split(values):
    first = values.astype(jnp.bfloat16).astype(jnp.float32)
    rest = values - first
    second = rest.astype(jnp.bfloat16).astype(jnp.float32)
    return first, second, rest - second


def features(points, weights):
    row = lax.broadcasted_iota(jnp.int32, (8, points.shape[1]), 0)
    x, y, z = (points[k : k + 1] - 0.5 for k in range(3))
    norm = x * x + y * y + z * z
    root = four_pi / weights
    scale = root * root
    shifted = jnp.where(row == 0, x, jnp.where(row == 1, y, z))
    left = jnp.where(row < 3, shifted, jnp.where(row == 3, norm, jnp.where(row == 4, 1.0, 0.0)))
    right = scale * jnp.where(
        row < 3,
        -2.0 * shifted,
        jnp.where(row == 3, 1.0, jnp.where(row == 4, norm + core_square, 0.0)),
    )
    a1, a2, a3 = split(left)
    b1, b2, b3 = split(right)
    return (
        jnp.concatenate([a1, a1, a2, a1, a3, a2], axis=0),
        jnp.concatenate([b1, b2, b1, b3, b1, b2], axis=0),
    )


def whole_kernel(
    sizes,
    offsets_any,
    lists_any,
    relay_any,
    refs_any,
    dens_any,
    points_any,
    weights_any,
    basis_any,
    transfer_any,
    coarse_coupling_any,
    coupling_any,
    out_ref,
    offsets_ref,
    lists_ref,
    relay_ref,
    refs_ref,
    dens_ref,
    points_ref,
    weights_ref,
    basis_ref,
    transfer_ref,
    coarse_coupling_ref,
    coupling_ref,
    packed_coupling,
    row_feat,
    col_feat,
    values,
    coeff,
    outgoing,
    listed_packed,
    coarse_packed,
    listed,
    coarse,
    local1,
    halo_dens,
    halo_points,
    halo_weights,
    load_sems,
    coupling_sems,
    halo_send,
    halo_recv,
    list_send,
    list_recv,
    inner_send,
    inner_recv,
    outer_send,
    outer_recv,
):
    n_gx, n_gy = sizes
    total = n_gx * n_gy
    me = lax.axis_index("gx") * n_gy + lax.axis_index("gy")
    leaf_count, rank, leaf_size = basis_ref.shape
    rhs = dens_ref.shape[0]
    slots, capacity = offsets_ref.shape[0], lists_ref.shape[0]
    far0, far1 = relay_ref.shape[1], refs_ref.shape[1]
    groups = leaf_count // CHILDREN
    half_slots = capacity // 2
    rim = REACH * leaf_size
    columns = leaf_count * leaf_size

    loads = [
        pltpu.make_async_copy(source, target, load_sems.at[k])
        for k, (source, target) in enumerate(
            [
                (lists_any, lists_ref),
                (dens_any, dens_ref),
                (basis_any, basis_ref),
                (transfer_any, transfer_ref),
                (points_any, points_ref),
                (weights_any, weights_ref),
                (offsets_any, offsets_ref),
                (refs_any, refs_ref),
                (relay_any, relay_ref),
                (coarse_coupling_any, coarse_coupling_ref),
            ]
        )
    ]
    for load in loads:
        load.start()

    def coupling_load(group):
        span = pl.ds(group * CHILDREN, CHILDREN)
        return pltpu.make_async_copy(
            coupling_any.at[span], coupling_ref.at[span], coupling_sems.at[group]
        )

    for group in range(groups):
        coupling_load(group).start()

    def place(index):
        return (index // n_gy, index % n_gy)

    barrier = pltpu.get_barrier_semaphore()

    def greet(step, carry):
        other = (me + step) % total
        pl.semaphore_signal(barrier, inc=1, device_id=place(other), device_id_type=MESH)
        return carry

    lax.fori_loop(1, total, greet, 0)
    for load in loads[:3]:
        load.wait()

    low = lax.broadcasted_iota(jnp.int32, (rhs, 2 * rank), 1) < rank

    def leaf_coefficients(step, carry):
        for k in range(CHILDREN):
            leaf = step * CHILDREN + k
            start = pl.multiple_of(leaf * leaf_size, leaf_size)
            basis = basis_ref[leaf]
            doubled = jnp.concatenate([basis, basis], axis=0)
            both = dot(dens_ref[:, pl.ds(start, leaf_size)], doubled, ROWS_BY_ROWS)
            coeff[leaf] = both.astype(jnp.bfloat16)
        return carry

    lax.fori_loop(0, groups, leaf_coefficients, 0, unroll=2)

    def gather(window):
        for slot in range(half_slots):
            first = coeff[lists_ref[slot, window]]
            second = coeff[lists_ref[slot + half_slots, window]]
            outgoing[window, slot] = jnp.where(low, first, second)

    def parent_coefficients(pair, carry):
        parents = []
        for g in range(2):
            parent = None
            for child in range(CHILDREN):
                leaf = (pair * 2 + g) * CHILDREN + child
                term = dot(coeff[leaf][:, :rank], transfer_ref[leaf], PLAIN)
                parent = term if parent is None else parent + term
            parents.append(parent)
        coarse_packed[me, pair] = jnp.concatenate(parents, axis=1).astype(jnp.bfloat16)
        return carry

    for load in loads[3:6]:
        load.wait()
    pl.semaphore_wait(barrier, total - 1)

    def halo(side):
        other = place(me - 1 if side == 0 else me + 1)
        start = 0 if side == 0 else columns - rim
        leaf = 0 if side == 0 else leaf_count - REACH
        parts = [
            (dens_ref.at[:, pl.ds(start, rim)], halo_dens),
            (points_ref.at[:, pl.ds(start, rim)], halo_points),
            (weights_ref.at[pl.ds(leaf, REACH)], halo_weights),
        ]
        return [
            pltpu.make_async_remote_copy(
                src_ref=source,
                dst_ref=target.at[1 - side],
                send_sem=halo_send.at[side, kind],
                recv_sem=halo_recv.at[1 - side, kind],
                device_id=other,
                device_id_type=MESH,
            )
            for kind, (source, target) in enumerate(parts)
        ]

    @pl.when(me > 0)
    def _():
        for copy in halo(0):
            copy.start()

    @pl.when(me < total - 1)
    def _():
        for copy in halo(1):
            copy.start()

    my_gx, my_gy = lax.axis_index("gx"), lax.axis_index("gy")

    def inner_copy(other, slot):
        block = coarse_packed.at[my_gx * n_gy + slot]
        return pltpu.make_async_remote_copy(
            src_ref=block,
            dst_ref=block,
            send_sem=inner_send.at[other],
            recv_sem=inner_recv.at[slot],
            device_id=(my_gx, other),
            device_id_type=MESH,
        )

    def outer_copy(other, slot):
        block = coarse_packed.at[pl.ds(slot * n_gy, n_gy)]
        return pltpu.make_async_remote_copy(
            src_ref=block,
            dst_ref=block,
            send_sem=outer_send.at[other],
            recv_sem=outer_recv.at[slot],
            device_id=(other, my_gy),
            device_id_type=MESH,
        )

    def list_copy(window, landing):
        return pltpu.make_async_remote_copy(
            src_ref=outgoing.at[window],
            dst_ref=listed_packed.at[landing],
            send_sem=list_send.at[window],
            recv_sem=list_recv.at[landing],
            device_id=place(me + window - WINDOW),
            device_id_type=MESH,
        )

    def in_window(window):
        other = me + window - WINDOW
        return (window != WINDOW) & (other >= 0) & (other < total)

    def send_list(window, carry):
        gather(window)

        @pl.when(in_window(window))
        def _():
            list_copy(window, 2 * WINDOW - window).start()

        return carry

    lax.fori_loop(0, WINDOWS, send_list, 0)
    listed_packed[WINDOW] = outgoing[WINDOW]
    lax.fori_loop(0, groups // 2, parent_coefficients, 0)

    def send_inner(step, carry):
        inner_copy((my_gy + step) % n_gy, my_gy).start()
        return carry

    lax.fori_loop(1, n_gy, send_inner, 0)

    for load in loads[6:9]:
        load.wait()
    batch = 4

    def prepare(first_leaf, points, weights, dens, own):
        line = jnp.concatenate([weights[k : k + 1] for k in range(batch)], axis=1)
        left, right = features(points, line)
        right = right.astype(jnp.bfloat16)
        for k in range(batch):
            part = slice(k * leaf_size, (k + 1) * leaf_size)
            col_feat[first_leaf + k] = right[:, part]
            values[first_leaf + k] = dens[:, part]
            if own:
                row_feat[first_leaf - REACH + k] = left[:, part].T.astype(jnp.bfloat16)

    def prepare_own(step, carry):
        span = pl.ds(pl.multiple_of(step * batch * leaf_size, batch * leaf_size), batch * leaf_size)
        lines = weights_ref[pl.ds(step * batch, batch)]
        prepare(REACH + step * batch, points_ref[:, span], lines, dens_ref[:, span], True)
        return carry

    lax.fori_loop(0, leaf_count // batch, prepare_own, 0)

    def near_leaf(leaf, carry):
        mine = row_feat[leaf]
        partners = [leaf + REACH + offsets_ref[slot, leaf] for slot in range(slots)]
        kernels = []
        for first in range(0, slots, 2):
            some = partners[first : first + 2]
            cols = jnp.concatenate([col_feat[p] for p in some], axis=1)
            kernels.append(lax.rsqrt(dot(mine, cols, PLAIN).astype(jnp.bfloat16)))
        vals = jnp.concatenate([values[p] for p in partners], axis=1)
        field = dot(jnp.concatenate(kernels, axis=1), vals, ROWS_BY_ROWS)
        out_ref[:, pl.ds(pl.multiple_of(leaf * leaf_size, leaf_size), leaf_size)] = field.T
        return carry

    middle = leaf_count // 2
    lax.fori_loop(REACH, middle, near_leaf, 0, unroll=2)

    def end_inner(step, carry):
        other = (my_gy + step) % n_gy
        inner_copy(other, other).wait_recv()
        inner_copy(other, my_gy).wait_send()
        return carry

    lax.fori_loop(1, n_gy, end_inner, 0)

    def send_outer(step, carry):
        outer_copy((my_gx + step) % n_gx, my_gx).start()
        return carry

    lax.fori_loop(1, n_gx, send_outer, 0)
    lax.fori_loop(middle, leaf_count - REACH, near_leaf, 0, unroll=2)

    @pl.when(me == 0)
    def _():
        halo_dens[0] = jnp.zeros(halo_dens.shape[1:], halo_dens.dtype)
        halo_points[0] = jnp.zeros(halo_points.shape[1:], halo_points.dtype)
        halo_weights[0] = jnp.ones(halo_weights.shape[1:], halo_weights.dtype)

    @pl.when(me == total - 1)
    def _():
        halo_dens[1] = jnp.zeros(halo_dens.shape[1:], halo_dens.dtype)
        halo_points[1] = jnp.zeros(halo_points.shape[1:], halo_points.dtype)
        halo_weights[1] = jnp.ones(halo_weights.shape[1:], halo_weights.dtype)

    @pl.when(me > 0)
    def _():
        for copy in halo(1):
            copy.wait_recv()
        for copy in halo(0):
            copy.wait_send()

    @pl.when(me < total - 1)
    def _():
        for copy in halo(0):
            copy.wait_recv()
        for copy in halo(1):
            copy.wait_send()

    for side in range(2):
        base = 0 if side == 0 else REACH + leaf_count

        def prepare_rim(step, carry, side=side, base=base):
            width = batch * leaf_size
            span = pl.ds(pl.multiple_of(step * width, width), width)
            lines = halo_weights[side, pl.ds(step * batch, batch)]
            dens = halo_dens[side, :, span]
            prepare(base + step * batch, halo_points[side, :, span], lines, dens, False)
            return carry

        lax.fori_loop(0, REACH // batch, prepare_rim, 0)

    lax.fori_loop(0, REACH, near_leaf, 0, unroll=2)
    lax.fori_loop(leaf_count - REACH, leaf_count, near_leaf, 0, unroll=2)

    def end_outer(step, carry):
        other = (my_gx + step) % n_gx
        outer_copy(other, other).wait_recv()
        outer_copy(other, my_gx).wait_send()
        return carry

    lax.fori_loop(1, n_gx, end_outer, 0)

    def opened(packed):
        both = packed.astype(jnp.float32)
        turned = pltpu.roll(both, rank, 1)
        return (
            jnp.where(low, both, turned).astype(jnp.bfloat16),
            jnp.where(low, turned, both).astype(jnp.bfloat16),
        )

    pairs = groups // 2

    def open_coarse(step, carry):
        for k in range(4 * pairs):
            first, second = opened(coarse_packed[step * 4 + k // pairs, k % pairs])
            index = step * 8 * pairs + 2 * k
            coarse[index] = first
            coarse[index + 1] = second
        return carry

    lax.fori_loop(0, total // 4, open_coarse, 0)
    loads[9].wait()

    def beside(blocks, count):
        return jnp.concatenate([blocks(slot) for slot in range(count)], axis=1)

    def couple(matrix, store, pick, count):
        taken = [store[pick(slot)] for slot in range(count)]
        picked = [jnp.where(low, taken[k], taken[k + 1]) for k in range(0, count, 2)]
        return dot(matrix, jnp.concatenate(picked, axis=1), ROWS_BY_ROWS)

    def one_group(group, carry):
        local1[group] = couple(
            beside(lambda s: coarse_coupling_ref[group, s], far1),
            coarse,
            lambda s: refs_ref[group, s],
            far1,
        ).astype(jnp.bfloat16)
        return carry

    lax.fori_loop(0, groups, one_group, 0, unroll=2)

    for group in range(groups):
        coupling_load(group).wait()

    def pack_leaf(leaf, carry):
        packed_coupling[leaf] = beside(lambda s: coupling_ref[leaf, s], far0)
        return carry

    lax.fori_loop(0, leaf_count, pack_leaf, 0)

    def end_list(window, carry):
        @pl.when(in_window(window))
        def _():
            list_copy(window, window).wait_recv()
            list_copy(window, 2 * WINDOW - window).wait_send()

        for slot in range(half_slots):
            first, second = opened(listed_packed[window, slot])
            index = window * capacity + slot
            listed[index] = first
            listed[index + half_slots] = second
        return carry

    lax.fori_loop(0, WINDOWS, end_list, 0)

    def one_leaf(leaf, carry):
        local0 = couple(
            packed_coupling[leaf],
            listed,
            lambda s: relay_ref[leaf, s],
            far0,
        )
        downward = dot(transfer_ref[leaf], local1[leaf // CHILDREN], PLAIN)
        field = (local0 + downward).T.astype(jnp.bfloat16)
        span = pl.ds(pl.multiple_of(leaf * leaf_size, leaf_size), leaf_size)
        out_ref[:, span] = out_ref[:, span] + dot(field, basis_ref[leaf], PLAIN)
        return carry

    lax.fori_loop(0, leaf_count, one_leaf, 0, unroll=2)


def whole(sizes, tables, densities, points, weights, leaf_basis, transfer, coarse_coupling, coupling):
    rhs, columns = densities.shape
    leaf_count, rank, leaf_size = leaf_basis.shape
    total = sizes[0] * sizes[1]
    groups = leaf_count // CHILDREN
    capacity = tables[1].shape[0]
    anywhere = pl.BlockSpec(memory_space=pl.ANY)
    rim = REACH * leaf_size
    dma = pltpu.SemaphoreType.DMA
    operands = (densities, points, weights, leaf_basis, transfer, coarse_coupling, coupling)
    held = [pltpu.SMEM(x.shape, x.dtype) for x in tables]
    held += [pltpu.VMEM(x.shape, x.dtype) for x in operands]
    half = jnp.bfloat16
    return pl.pallas_call(
        functools.partial(whole_kernel, sizes),
        out_shape=jax.ShapeDtypeStruct((rhs, columns), jnp.float32),
        in_specs=[anywhere] * (len(tables) + len(operands)),
        out_specs=pl.BlockSpec(memory_space=pltpu.VMEM),
        scratch_shapes=held
        + [
            pltpu.VMEM((leaf_count, rank, coupling.shape[1] * rank), half),
            pltpu.VMEM((leaf_count, leaf_size, 48), half),
            pltpu.VMEM((leaf_count + 2 * REACH, 48, leaf_size), half),
            pltpu.VMEM((leaf_count + 2 * REACH, rhs, leaf_size), half),
            pltpu.VMEM((leaf_count, rhs, 2 * rank), half),
            pltpu.VMEM((WINDOWS, capacity // 2, rhs, 2 * rank), half),
            pltpu.VMEM((WINDOWS, capacity // 2, rhs, 2 * rank), half),
            pltpu.VMEM((total, groups // 2, rhs, 2 * rank), half),
            pltpu.VMEM((WINDOWS * capacity, rhs, 2 * rank), half),
            pltpu.VMEM((total * groups, rhs, 2 * rank), half),
            pltpu.VMEM((groups, rank, rhs), half),
            pltpu.VMEM((2, rhs, rim), half),
            pltpu.VMEM((2, 3, rim), jnp.float32),
            pltpu.VMEM((2, REACH, leaf_size), jnp.float32),
            dma((10,)),
            dma((groups,)),
            dma((2, 3)),
            dma((2, 3)),
            dma((WINDOWS,)),
            dma((WINDOWS,)),
            dma((sizes[1],)),
            dma((sizes[1],)),
            dma((sizes[0],)),
            dma((sizes[0],)),
        ],
        compiler_params=pltpu.CompilerParams(
            collective_id=0, has_side_effects=True, vmem_limit_bytes=63 * 1024 * 1024
        ),
        name="whole",
    )(*tables, *operands)


def local(
    sizes,
    densities,
    points,
    weights,
    near_offsets,
    leaf_basis,
    transfer,
    send_lists,
    relay_refs,
    leaf_coupling,
    coarse_refs,
    coarse_coupling,
):
    leaf_count, _, leaf_size = leaf_basis.shape
    lines = weights.reshape(leaf_count, leaf_size)
    tables = (near_offsets.T, send_lists[0].T, relay_refs, coarse_refs)
    return whole(
        sizes,
        tables,
        densities,
        points,
        lines,
        leaf_basis,
        transfer,
        coarse_coupling,
        leaf_coupling,
    )


def solution(mesh):
    sizes = (mesh.shape["gx"], mesh.shape["gy"])
    in_specs = (
        P(None, ("gx", "gy")),
        P(None, ("gx", "gy")),
        P(("gx", "gy")),
        P(("gx", "gy"), None),
        P(("gx", "gy"), None, None),
        P(("gx", "gy"), None, None),
        P(("gx", "gy"), None, None),
        P(("gx", "gy"), None),
        P(("gx", "gy"), None, None, None),
        P(("gx", "gy"), None),
        P(("gx", "gy"), None, None, None),
    )
    out_specs = P(None, ("gx", "gy"))
    return jax.shard_map(
        functools.partial(local, sizes),
        mesh=mesh,
        in_specs=in_specs,
        out_specs=out_specs,
        check_vma=False,
    )
```

```python
import functools
import math

import jax
import jax.numpy as jnp
from jax import lax
from jax.experimental import pallas as pl
from jax.experimental.pallas import tpu as pltpu
from jax.sharding import PartitionSpec as P

REACH = 8
WINDOW = 8
CHILDREN = 8
WINDOWS = 2 * WINDOW + 1

core_square = 0.0004
four_pi = 4.0 * math.pi

MESH = pl.DeviceIdType.MESH
ROWS_BY_ROWS = (((1,), (1,)), ((), ()))
PLAIN = (((1,), (0,)), ((), ()))


def dot(left, right, dims):
    return lax.dot_general(left, right, dims, preferred_element_type=jnp.float32)


def split(values):
    first = values.astype(jnp.bfloat16).astype(jnp.float32)
    rest = values - first
    second = rest.astype(jnp.bfloat16).astype(jnp.float32)
    return first, second, rest - second


def features(points, weights):
    row = lax.broadcasted_iota(jnp.int32, (8, points.shape[1]), 0)
    x, y, z = (points[k : k + 1] - 0.5 for k in range(3))
    norm = x * x + y * y + z * z
    root = four_pi / weights
    scale = root * root
    shifted = jnp.where(row == 0, x, jnp.where(row == 1, y, z))
    left = jnp.where(row < 3, shifted, jnp.where(row == 3, norm, jnp.where(row == 4, 1.0, 0.0)))
    right = scale * jnp.where(
        row < 3,
        -2.0 * shifted,
        jnp.where(row == 3, 1.0, jnp.where(row == 4, norm + core_square, 0.0)),
    )
    a1, a2, a3 = split(left)
    b1, b2, b3 = split(right)
    return (
        jnp.concatenate([a1, a1, a2, a1, a3, a2], axis=0),
        jnp.concatenate([b1, b2, b1, b3, b1, b2], axis=0),
    )


def whole_kernel(
    sizes,
    offsets_any,
    lists_any,
    relay_any,
    refs_any,
    dens_any,
    points_any,
    weights_any,
    basis_any,
    transfer_any,
    coarse_coupling_any,
    coupling_any,
    out_ref,
    offsets_ref,
    lists_ref,
    relay_ref,
    refs_ref,
    dens_ref,
    points_ref,
    weights_ref,
    basis_ref,
    transfer_ref,
    coarse_coupling_ref,
    coupling_ref,
    row_feat,
    col_feat,
    values,
    coeff,
    outgoing,
    listed_packed,
    coarse_packed,
    listed,
    coarse,
    local1,
    halo_dens,
    halo_points,
    halo_weights,
    load_sems,
    coupling_sems,
    halo_send,
    halo_recv,
    list_send,
    list_recv,
    inner_send,
    inner_recv,
    outer_send,
    outer_recv,
):
    n_gx, n_gy = sizes
    total = n_gx * n_gy
    me = lax.axis_index("gx") * n_gy + lax.axis_index("gy")
    leaf_count, rank, leaf_size = basis_ref.shape
    rhs = dens_ref.shape[0]
    slots, capacity = offsets_ref.shape[0], lists_ref.shape[0]
    far0, far1 = relay_ref.shape[1], refs_ref.shape[1]
    groups = leaf_count // CHILDREN
    half_slots = capacity // 2
    rim = REACH * leaf_size
    columns = leaf_count * leaf_size

    loads = [
        pltpu.make_async_copy(source, target, load_sems.at[k])
        for k, (source, target) in enumerate(
            [
                (lists_any, lists_ref),
                (dens_any, dens_ref),
                (basis_any, basis_ref),
                (transfer_any, transfer_ref),
                (points_any, points_ref),
                (weights_any, weights_ref),
                (offsets_any, offsets_ref),
                (refs_any, refs_ref),
                (relay_any, relay_ref),
                (coarse_coupling_any, coarse_coupling_ref),
            ]
        )
    ]
    for load in loads:
        load.start()

    def coupling_load(group):
        span = pl.ds(group * CHILDREN, CHILDREN)
        return pltpu.make_async_copy(
            coupling_any.at[span], coupling_ref.at[span], coupling_sems.at[group]
        )

    for group in range(groups):
        coupling_load(group).start()

    def place(index):
        return (index // n_gy, index % n_gy)

    barrier = pltpu.get_barrier_semaphore()

    def greet(step, carry):
        other = (me + step) % total
        pl.semaphore_signal(barrier, inc=1, device_id=place(other), device_id_type=MESH)
        return carry

    lax.fori_loop(1, total, greet, 0)
    for load in loads[:3]:
        load.wait()

    low = lax.broadcasted_iota(jnp.int32, (rhs, 2 * rank), 1) < rank

    def leaf_coefficients(step, carry):
        for k in range(CHILDREN):
            leaf = step * CHILDREN + k
            start = pl.multiple_of(leaf * leaf_size, leaf_size)
            basis = basis_ref[leaf]
            doubled = jnp.concatenate([basis, basis], axis=0)
            both = dot(dens_ref[:, pl.ds(start, leaf_size)], doubled, ROWS_BY_ROWS)
            coeff[leaf] = both.astype(jnp.bfloat16)
        return carry

    lax.fori_loop(0, groups, leaf_coefficients, 0, unroll=2)

    def gather(window):
        for slot in range(half_slots):
            first = coeff[lists_ref[slot, window]]
            second = coeff[lists_ref[slot + half_slots, window]]
            outgoing[window, slot] = jnp.where(low, first, second)

    def parent_coefficients(pair, carry):
        parents = []
        for g in range(2):
            parent = None
            for child in range(CHILDREN):
                leaf = (pair * 2 + g) * CHILDREN + child
                term = dot(coeff[leaf][:, :rank], transfer_ref[leaf], PLAIN)
                parent = term if parent is None else parent + term
            parents.append(parent)
        coarse_packed[me, pair] = jnp.concatenate(parents, axis=1).astype(jnp.bfloat16)
        return carry

    for load in loads[3:6]:
        load.wait()
    pl.semaphore_wait(barrier, total - 1)

    def halo(side):
        other = place(me - 1 if side == 0 else me + 1)
        start = 0 if side == 0 else columns - rim
        leaf = 0 if side == 0 else leaf_count - REACH
        parts = [
            (dens_ref.at[:, pl.ds(start, rim)], halo_dens),
            (points_ref.at[:, pl.ds(start, rim)], halo_points),
            (weights_ref.at[pl.ds(leaf, REACH)], halo_weights),
        ]
        return [
            pltpu.make_async_remote_copy(
                src_ref=source,
                dst_ref=target.at[1 - side],
                send_sem=halo_send.at[side, kind],
                recv_sem=halo_recv.at[1 - side, kind],
                device_id=other,
                device_id_type=MESH,
            )
            for kind, (source, target) in enumerate(parts)
        ]

    @pl.when(me > 0)
    def _():
        for copy in halo(0):
            copy.start()

    @pl.when(me < total - 1)
    def _():
        for copy in halo(1):
            copy.start()

    my_gx, my_gy = lax.axis_index("gx"), lax.axis_index("gy")

    def inner_copy(other, slot):
        block = coarse_packed.at[my_gx * n_gy + slot]
        return pltpu.make_async_remote_copy(
            src_ref=block,
            dst_ref=block,
            send_sem=inner_send.at[other],
            recv_sem=inner_recv.at[slot],
            device_id=(my_gx, other),
            device_id_type=MESH,
        )

    def outer_copy(other, slot):
        block = coarse_packed.at[pl.ds(slot * n_gy, n_gy)]
        return pltpu.make_async_remote_copy(
            src_ref=block,
            dst_ref=block,
            send_sem=outer_send.at[other],
            recv_sem=outer_recv.at[slot],
            device_id=(other, my_gy),
            device_id_type=MESH,
        )

    def list_copy(window, landing):
        return pltpu.make_async_remote_copy(
            src_ref=outgoing.at[window],
            dst_ref=listed_packed.at[landing],
            send_sem=list_send.at[window],
            recv_sem=list_recv.at[landing],
            device_id=place(me + window - WINDOW),
            device_id_type=MESH,
        )

    def in_window(window):
        other = me + window - WINDOW
        return (window != WINDOW) & (other >= 0) & (other < total)

    def send_list(window, carry):
        gather(window)

        @pl.when(in_window(window))
        def _():
            list_copy(window, 2 * WINDOW - window).start()

        return carry

    lax.fori_loop(0, WINDOWS, send_list, 0)
    listed_packed[WINDOW] = outgoing[WINDOW]
    lax.fori_loop(0, groups // 2, parent_coefficients, 0)

    def send_inner(step, carry):
        inner_copy((my_gy + step) % n_gy, my_gy).start()
        return carry

    lax.fori_loop(1, n_gy, send_inner, 0)

    for load in loads[6:9]:
        load.wait()
    batch = 4

    def prepare(first_leaf, points, weights, dens, own):
        line = jnp.concatenate([weights[k : k + 1] for k in range(batch)], axis=1)
        left, right = features(points, line)
        right = right.astype(jnp.bfloat16)
        for k in range(batch):
            part = slice(k * leaf_size, (k + 1) * leaf_size)
            col_feat[first_leaf + k] = right[:, part]
            values[first_leaf + k] = dens[:, part]
            if own:
                row_feat[first_leaf - REACH + k] = left[:, part].T.astype(jnp.bfloat16)

    def prepare_own(step, carry):
        span = pl.ds(pl.multiple_of(step * batch * leaf_size, batch * leaf_size), batch * leaf_size)
        lines = weights_ref[pl.ds(step * batch, batch)]
        prepare(REACH + step * batch, points_ref[:, span], lines, dens_ref[:, span], True)
        return carry

    lax.fori_loop(0, leaf_count // batch, prepare_own, 0)

    def near_leaf(leaf, carry):
        mine = row_feat[leaf]
        partners = [leaf + REACH + offsets_ref[slot, leaf] for slot in range(slots)]
        kernels = []
        for first in range(0, slots, 2):
            some = partners[first : first + 2]
            cols = jnp.concatenate([col_feat[p] for p in some], axis=1)
            kernels.append(lax.rsqrt(dot(mine, cols, PLAIN).astype(jnp.bfloat16)))
        vals = jnp.concatenate([values[p] for p in partners], axis=1)
        field = dot(jnp.concatenate(kernels, axis=1), vals, ROWS_BY_ROWS)
        out_ref[:, pl.ds(pl.multiple_of(leaf * leaf_size, leaf_size), leaf_size)] = field.T
        return carry

    middle = leaf_count // 2
    lax.fori_loop(REACH, middle, near_leaf, 0, unroll=2)

    def end_inner(step, carry):
        other = (my_gy + step) % n_gy
        inner_copy(other, other).wait_recv()
        inner_copy(other, my_gy).wait_send()
        return carry

    lax.fori_loop(1, n_gy, end_inner, 0)

    def send_outer(step, carry):
        outer_copy((my_gx + step) % n_gx, my_gx).start()
        return carry

    lax.fori_loop(1, n_gx, send_outer, 0)
    lax.fori_loop(middle, leaf_count - REACH, near_leaf, 0, unroll=2)

    @pl.when(me == 0)
    def _():
        halo_dens[0] = jnp.zeros(halo_dens.shape[1:], halo_dens.dtype)
        halo_points[0] = jnp.zeros(halo_points.shape[1:], halo_points.dtype)
        halo_weights[0] = jnp.ones(halo_weights.shape[1:], halo_weights.dtype)

    @pl.when(me == total - 1)
    def _():
        halo_dens[1] = jnp.zeros(halo_dens.shape[1:], halo_dens.dtype)
        halo_points[1] = jnp.zeros(halo_points.shape[1:], halo_points.dtype)
        halo_weights[1] = jnp.ones(halo_weights.shape[1:], halo_weights.dtype)

    @pl.when(me > 0)
    def _():
        for copy in halo(1):
            copy.wait_recv()
        for copy in halo(0):
            copy.wait_send()

    @pl.when(me < total - 1)
    def _():
        for copy in halo(0):
            copy.wait_recv()
        for copy in halo(1):
            copy.wait_send()

    for side in range(2):
        base = 0 if side == 0 else REACH + leaf_count

        def prepare_rim(step, carry, side=side, base=base):
            width = batch * leaf_size
            span = pl.ds(pl.multiple_of(step * width, width), width)
            lines = halo_weights[side, pl.ds(step * batch, batch)]
            dens = halo_dens[side, :, span]
            prepare(base + step * batch, halo_points[side, :, span], lines, dens, False)
            return carry

        lax.fori_loop(0, REACH // batch, prepare_rim, 0)

    lax.fori_loop(0, REACH, near_leaf, 0, unroll=2)
    lax.fori_loop(leaf_count - REACH, leaf_count, near_leaf, 0, unroll=2)

    def end_outer(step, carry):
        other = (my_gx + step) % n_gx
        outer_copy(other, other).wait_recv()
        outer_copy(other, my_gx).wait_send()
        return carry

    lax.fori_loop(1, n_gx, end_outer, 0)

    def opened(packed):
        both = packed.astype(jnp.float32)
        turned = pltpu.roll(both, rank, 1)
        return (
            jnp.where(low, both, turned).astype(jnp.bfloat16),
            jnp.where(low, turned, both).astype(jnp.bfloat16),
        )

    pairs = groups // 2

    def open_coarse(step, carry):
        for k in range(4 * pairs):
            first, second = opened(coarse_packed[step * 4 + k // pairs, k % pairs])
            index = step * 8 * pairs + 2 * k
            coarse[index] = first
            coarse[index + 1] = second
        return carry

    lax.fori_loop(0, total // 4, open_coarse, 0)
    loads[9].wait()

    def couple(blocks, store, pick, count):
        crossed = None
        for slot in range(0, count, 4):
            matrix = blocks(slot).reshape(4 * rank, rank)
            picked = jnp.concatenate([store[pick(slot + k)] for k in range(4)], axis=0)
            term = dot(picked[:, :rank], matrix, ROWS_BY_ROWS)
            crossed = term if crossed is None else crossed + term
        both = jnp.zeros((rhs, 2 * rank), jnp.float32)
        for k in range(0, 4, 2):
            lanes = slice(k * rank, (k + 2) * rank)
            upper = crossed[k * rhs : (k + 1) * rhs, lanes]
            lower = crossed[(k + 1) * rhs : (k + 2) * rhs, lanes]
            both = both + jnp.where(low, upper, lower)
        return both[:, :rank] + both[:, rank:]

    def one_group(group, carry):
        local1[group] = couple(
            lambda s: coarse_coupling_ref[group, pl.ds(s, 4)],
            coarse,
            lambda s: refs_ref[group, s],
            far1,
        ).astype(jnp.bfloat16)
        return carry

    lax.fori_loop(0, groups, one_group, 0, unroll=2)

    for group in range(groups):
        coupling_load(group).wait()

    def end_list(window, carry):
        @pl.when(in_window(window))
        def _():
            list_copy(window, window).wait_recv()
            list_copy(window, 2 * WINDOW - window).wait_send()

        for slot in range(half_slots):
            first, second = opened(listed_packed[window, slot])
            index = window * capacity + slot
            listed[index] = first
            listed[index + half_slots] = second
        return carry

    lax.fori_loop(0, WINDOWS, end_list, 0)

    def one_leaf(leaf, carry):
        local0 = couple(
            lambda s: coupling_ref[leaf, pl.ds(s, 4)],
            listed,
            lambda s: relay_ref[leaf, s],
            far0,
        )
        downward = dot(local1[leaf // CHILDREN], transfer_ref[leaf], ROWS_BY_ROWS)
        field = (local0 + downward).astype(jnp.bfloat16)
        span = pl.ds(pl.multiple_of(leaf * leaf_size, leaf_size), leaf_size)
        out_ref[:, span] = out_ref[:, span] + dot(field, basis_ref[leaf], PLAIN)
        return carry

    lax.fori_loop(0, leaf_count, one_leaf, 0, unroll=2)


def whole(sizes, tables, densities, points, weights, leaf_basis, transfer, coarse_coupling, coupling):
    rhs, columns = densities.shape
    leaf_count, rank, leaf_size = leaf_basis.shape
    total = sizes[0] * sizes[1]
    groups = leaf_count // CHILDREN
    capacity = tables[1].shape[0]
    anywhere = pl.BlockSpec(memory_space=pl.ANY)
    rim = REACH * leaf_size
    dma = pltpu.SemaphoreType.DMA
    operands = (densities, points, weights, leaf_basis, transfer, coarse_coupling, coupling)
    held = [pltpu.SMEM(x.shape, x.dtype) for x in tables]
    held += [pltpu.VMEM(x.shape, x.dtype) for x in operands]
    half = jnp.bfloat16
    return pl.pallas_call(
        functools.partial(whole_kernel, sizes),
        out_shape=jax.ShapeDtypeStruct((rhs, columns), jnp.float32),
        in_specs=[anywhere] * (len(tables) + len(operands)),
        out_specs=pl.BlockSpec(memory_space=pltpu.VMEM),
        scratch_shapes=held
        + [
            pltpu.VMEM((leaf_count, leaf_size, 48), half),
            pltpu.VMEM((leaf_count + 2 * REACH, 48, leaf_size), half),
            pltpu.VMEM((leaf_count + 2 * REACH, rhs, leaf_size), half),
            pltpu.VMEM((leaf_count, rhs, 2 * rank), half),
            pltpu.VMEM((WINDOWS, capacity // 2, rhs, 2 * rank), half),
            pltpu.VMEM((WINDOWS, capacity // 2, rhs, 2 * rank), half),
            pltpu.VMEM((total, groups // 2, rhs, 2 * rank), half),
            pltpu.VMEM((WINDOWS * capacity, rhs, 2 * rank), half),
            pltpu.VMEM((total * groups, rhs, 2 * rank), half),
            pltpu.VMEM((groups, rhs, rank), half),
            pltpu.VMEM((2, rhs, rim), half),
            pltpu.VMEM((2, 3, rim), jnp.float32),
            pltpu.VMEM((2, REACH, leaf_size), jnp.float32),
            dma((10,)),
            dma((groups,)),
            dma((2, 3)),
            dma((2, 3)),
            dma((WINDOWS,)),
            dma((WINDOWS,)),
            dma((sizes[1],)),
            dma((sizes[1],)),
            dma((sizes[0],)),
            dma((sizes[0],)),
        ],
        compiler_params=pltpu.CompilerParams(
            collective_id=0, has_side_effects=True, vmem_limit_bytes=63 * 1024 * 1024
        ),
        name="whole",
    )(*tables, *operands)


def local(
    sizes,
    densities,
    points,
    weights,
    near_offsets,
    leaf_basis,
    transfer,
    send_lists,
    relay_refs,
    leaf_coupling,
    coarse_refs,
    coarse_coupling,
):
    leaf_count, _, leaf_size = leaf_basis.shape
    lines = weights.reshape(leaf_count, leaf_size)
    tables = (near_offsets.T, send_lists[0].T, relay_refs, coarse_refs)
    return whole(
        sizes,
        tables,
        densities,
        points,
        lines,
        leaf_basis,
        transfer,
        coarse_coupling,
        leaf_coupling,
    )


def solution(mesh):
    sizes = (mesh.shape["gx"], mesh.shape["gy"])
    in_specs = (
        P(None, ("gx", "gy")),
        P(None, ("gx", "gy")),
        P(("gx", "gy")),
        P(("gx", "gy"), None),
        P(("gx", "gy"), None, None),
        P(("gx", "gy"), None, None),
        P(("gx", "gy"), None, None),
        P(("gx", "gy"), None),
        P(("gx", "gy"), None, None, None),
        P(("gx", "gy"), None),
        P(("gx", "gy"), None, None, None),
    )
    out_specs = P(None, ("gx", "gy"))
    return jax.shard_map(
        functools.partial(local, sizes),
        mesh=mesh,
        in_specs=in_specs,
        out_specs=out_specs,
        check_vma=False,
    )
```

```python
import functools
import math

import jax
import jax.numpy as jnp
from jax import lax
from jax.experimental import pallas as pl
from jax.experimental.pallas import tpu as pltpu
from jax.sharding import PartitionSpec as P

REACH = 8
WINDOW = 8
CHILDREN = 8
WINDOWS = 2 * WINDOW + 1

core_square = 0.0004
four_pi = 4.0 * math.pi

MESH = pl.DeviceIdType.MESH
ROWS_BY_ROWS = (((1,), (1,)), ((), ()))
PLAIN = (((1,), (0,)), ((), ()))


def dot(left, right, dims):
    return lax.dot_general(left, right, dims, preferred_element_type=jnp.float32)


def split(values):
    first = values.astype(jnp.bfloat16).astype(jnp.float32)
    rest = values - first
    second = rest.astype(jnp.bfloat16).astype(jnp.float32)
    return first, second, rest - second


def features(points, weights):
    row = lax.broadcasted_iota(jnp.int32, (8, points.shape[1]), 0)
    x, y, z = (points[k : k + 1] - 0.5 for k in range(3))
    norm = x * x + y * y + z * z
    root = four_pi / weights
    scale = root * root
    shifted = jnp.where(row == 0, x, jnp.where(row == 1, y, z))
    left = jnp.where(row < 3, shifted, jnp.where(row == 3, norm, jnp.where(row == 4, 1.0, 0.0)))
    right = scale * jnp.where(
        row < 3,
        -2.0 * shifted,
        jnp.where(row == 3, 1.0, jnp.where(row == 4, norm + core_square, 0.0)),
    )
    a1, a2, a3 = split(left)
    b1, b2, b3 = split(right)
    return (
        jnp.concatenate([a1, a1, a2, a1, a3, a2], axis=0),
        jnp.concatenate([b1, b2, b1, b3, b1, b2], axis=0),
    )


def whole_kernel(
    sizes,
    offsets_any,
    lists_any,
    relay_any,
    refs_any,
    dens_any,
    points_any,
    weights_any,
    basis_any,
    transfer_any,
    coarse_coupling_any,
    coupling_any,
    out_ref,
    offsets_ref,
    lists_ref,
    relay_ref,
    refs_ref,
    dens_ref,
    points_ref,
    weights_ref,
    basis_ref,
    transfer_ref,
    coarse_coupling_ref,
    coupling_ref,
    row_feat,
    col_feat,
    values,
    coeff,
    outgoing,
    listed_packed,
    coarse_packed,
    listed,
    coarse,
    local1,
    halo_dens,
    halo_points,
    halo_weights,
    load_sems,
    coupling_sems,
    halo_send,
    halo_recv,
    list_send,
    list_recv,
    inner_send,
    inner_recv,
    outer_send,
    outer_recv,
):
    n_gx, n_gy = sizes
    total = n_gx * n_gy
    me = lax.axis_index("gx") * n_gy + lax.axis_index("gy")
    leaf_count, rank, leaf_size = basis_ref.shape
    rhs = dens_ref.shape[0]
    slots, capacity = offsets_ref.shape[0], lists_ref.shape[0]
    far0, far1 = relay_ref.shape[1], refs_ref.shape[1]
    groups = leaf_count // CHILDREN
    half_slots = capacity // 2
    rim = REACH * leaf_size
    columns = leaf_count * leaf_size

    loads = [
        pltpu.make_async_copy(source, target, load_sems.at[k])
        for k, (source, target) in enumerate(
            [
                (lists_any, lists_ref),
                (dens_any, dens_ref),
                (basis_any, basis_ref),
                (transfer_any, transfer_ref),
                (points_any, points_ref),
                (weights_any, weights_ref),
                (offsets_any, offsets_ref),
                (refs_any, refs_ref),
                (relay_any, relay_ref),
                (coarse_coupling_any, coarse_coupling_ref),
            ]
        )
    ]
    for load in loads:
        load.start()

    def coupling_load(group):
        span = pl.ds(group * CHILDREN, CHILDREN)
        return pltpu.make_async_copy(
            coupling_any.at[span], coupling_ref.at[span], coupling_sems.at[group]
        )

    for group in range(groups):
        coupling_load(group).start()

    def place(index):
        return (index // n_gy, index % n_gy)

    barrier = pltpu.get_barrier_semaphore()

    def greet(step, carry):
        other = (me + step) % total
        pl.semaphore_signal(barrier, inc=1, device_id=place(other), device_id_type=MESH)
        return carry

    lax.fori_loop(1, total, greet, 0)
    for load in loads[:3]:
        load.wait()

    low = lax.broadcasted_iota(jnp.int32, (rhs, 2 * rank), 1) < rank

    def leaf_coefficients(step, carry):
        for k in range(CHILDREN):
            leaf = step * CHILDREN + k
            start = pl.multiple_of(leaf * leaf_size, leaf_size)
            basis = basis_ref[leaf]
            doubled = jnp.concatenate([basis, basis], axis=0)
            both = dot(dens_ref[:, pl.ds(start, leaf_size)], doubled, ROWS_BY_ROWS)
            coeff[leaf] = both.astype(jnp.bfloat16)
        return carry

    lax.fori_loop(0, groups, leaf_coefficients, 0, unroll=2)

    def gather(window):
        for slot in range(half_slots):
            first = coeff[lists_ref[slot, window]]
            second = coeff[lists_ref[slot + half_slots, window]]
            outgoing[window, slot] = jnp.where(low, first, second)

    def parent_coefficients(pair, carry):
        parents = []
        for g in range(2):
            parent = None
            for child in range(CHILDREN):
                leaf = (pair * 2 + g) * CHILDREN + child
                term = dot(coeff[leaf][:, :rank], transfer_ref[leaf], PLAIN)
                parent = term if parent is None else parent + term
            parents.append(parent)
        coarse_packed[me, pair] = jnp.concatenate(parents, axis=1).astype(jnp.bfloat16)
        return carry

    for load in loads[3:6]:
        load.wait()
    lax.fori_loop(0, groups // 2, parent_coefficients, 0)
    pl.semaphore_wait(barrier, total - 1)

    def halo(side):
        other = place(me - 1 if side == 0 else me + 1)
        start = 0 if side == 0 else columns - rim
        leaf = 0 if side == 0 else leaf_count - REACH
        parts = [
            (dens_ref.at[:, pl.ds(start, rim)], halo_dens),
            (points_ref.at[:, pl.ds(start, rim)], halo_points),
            (weights_ref.at[pl.ds(leaf, REACH)], halo_weights),
        ]
        return [
            pltpu.make_async_remote_copy(
                src_ref=source,
                dst_ref=target.at[1 - side],
                send_sem=halo_send.at[side, kind],
                recv_sem=halo_recv.at[1 - side, kind],
                device_id=other,
                device_id_type=MESH,
            )
            for kind, (source, target) in enumerate(parts)
        ]

    @pl.when(me > 0)
    def _():
        for copy in halo(0):
            copy.start()

    @pl.when(me < total - 1)
    def _():
        for copy in halo(1):
            copy.start()

    my_gx, my_gy = lax.axis_index("gx"), lax.axis_index("gy")

    def inner_copy(other, slot):
        block = coarse_packed.at[my_gx * n_gy + slot]
        return pltpu.make_async_remote_copy(
            src_ref=block,
            dst_ref=block,
            send_sem=inner_send.at[other],
            recv_sem=inner_recv.at[slot],
            device_id=(my_gx, other),
            device_id_type=MESH,
        )

    def outer_copy(other, slot):
        block = coarse_packed.at[pl.ds(slot * n_gy, n_gy)]
        return pltpu.make_async_remote_copy(
            src_ref=block,
            dst_ref=block,
            send_sem=outer_send.at[other],
            recv_sem=outer_recv.at[slot],
            device_id=(other, my_gy),
            device_id_type=MESH,
        )

    def list_copy(window, landing):
        return pltpu.make_async_remote_copy(
            src_ref=outgoing.at[window],
            dst_ref=listed_packed.at[landing],
            send_sem=list_send.at[window],
            recv_sem=list_recv.at[landing],
            device_id=place(me + window - WINDOW),
            device_id_type=MESH,
        )

    def in_window(window):
        other = me + window - WINDOW
        return (window != WINDOW) & (other >= 0) & (other < total)

    def send_list(window, carry):
        gather(window)

        @pl.when(in_window(window))
        def _():
            list_copy(window, 2 * WINDOW - window).start()

        return carry

    def send_inner(step, carry):
        inner_copy((my_gy + step) % n_gy, my_gy).start()
        return carry

    lax.fori_loop(1, n_gy, send_inner, 0)
    lax.fori_loop(0, WINDOWS, send_list, 0)
    listed_packed[WINDOW] = outgoing[WINDOW]

    for load in loads[6:9]:
        load.wait()
    batch = 4

    def prepare(first_leaf, points, weights, dens, own):
        line = jnp.concatenate([weights[k : k + 1] for k in range(batch)], axis=1)
        left, right = features(points, line)
        right = right.astype(jnp.bfloat16)
        for k in range(batch):
            part = slice(k * leaf_size, (k + 1) * leaf_size)
            col_feat[first_leaf + k] = right[:, part]
            values[first_leaf + k] = dens[:, part]
            if own:
                row_feat[first_leaf - REACH + k] = left[:, part].T.astype(jnp.bfloat16)

    def prepare_own(step, carry):
        span = pl.ds(pl.multiple_of(step * batch * leaf_size, batch * leaf_size), batch * leaf_size)
        lines = weights_ref[pl.ds(step * batch, batch)]
        prepare(REACH + step * batch, points_ref[:, span], lines, dens_ref[:, span], True)
        return carry

    lax.fori_loop(0, leaf_count // batch, prepare_own, 0)

    def near_leaf(leaf, carry):
        mine = row_feat[leaf]
        partners = [leaf + REACH + offsets_ref[slot, leaf] for slot in range(slots)]
        kernels = []
        for first in range(0, slots, 2):
            some = partners[first : first + 2]
            cols = jnp.concatenate([col_feat[p] for p in some], axis=1)
            kernels.append(lax.rsqrt(dot(mine, cols, PLAIN).astype(jnp.bfloat16)))
        vals = jnp.concatenate([values[p] for p in partners], axis=1)
        field = dot(jnp.concatenate(kernels, axis=1), vals, ROWS_BY_ROWS)
        out_ref[:, pl.ds(pl.multiple_of(leaf * leaf_size, leaf_size), leaf_size)] = field.T
        return carry

    middle = leaf_count // 2
    lax.fori_loop(REACH, middle, near_leaf, 0, unroll=2)

    def end_inner(step, carry):
        other = (my_gy + step) % n_gy
        inner_copy(other, other).wait_recv()
        inner_copy(other, my_gy).wait_send()
        return carry

    lax.fori_loop(1, n_gy, end_inner, 0)

    def send_outer(step, carry):
        outer_copy((my_gx + step) % n_gx, my_gx).start()
        return carry

    lax.fori_loop(1, n_gx, send_outer, 0)
    lax.fori_loop(middle, leaf_count - REACH, near_leaf, 0, unroll=2)

    @pl.when(me == 0)
    def _():
        halo_dens[0] = jnp.zeros(halo_dens.shape[1:], halo_dens.dtype)
        halo_points[0] = jnp.zeros(halo_points.shape[1:], halo_points.dtype)
        halo_weights[0] = jnp.ones(halo_weights.shape[1:], halo_weights.dtype)

    @pl.when(me == total - 1)
    def _():
        halo_dens[1] = jnp.zeros(halo_dens.shape[1:], halo_dens.dtype)
        halo_points[1] = jnp.zeros(halo_points.shape[1:], halo_points.dtype)
        halo_weights[1] = jnp.ones(halo_weights.shape[1:], halo_weights.dtype)

    @pl.when(me > 0)
    def _():
        for copy in halo(1):
            copy.wait_recv()
        for copy in halo(0):
            copy.wait_send()

    @pl.when(me < total - 1)
    def _():
        for copy in halo(0):
            copy.wait_recv()
        for copy in halo(1):
            copy.wait_send()

    for side in range(2):
        base = 0 if side == 0 else REACH + leaf_count

        def prepare_rim(step, carry, side=side, base=base):
            width = batch * leaf_size
            span = pl.ds(pl.multiple_of(step * width, width), width)
            lines = halo_weights[side, pl.ds(step * batch, batch)]
            dens = halo_dens[side, :, span]
            prepare(base + step * batch, halo_points[side, :, span], lines, dens, False)
            return carry

        lax.fori_loop(0, REACH // batch, prepare_rim, 0)

    lax.fori_loop(0, REACH, near_leaf, 0, unroll=2)
    lax.fori_loop(leaf_count - REACH, leaf_count, near_leaf, 0, unroll=2)

    def end_outer(step, carry):
        other = (my_gx + step) % n_gx
        outer_copy(other, other).wait_recv()
        outer_copy(other, my_gx).wait_send()
        return carry

    lax.fori_loop(1, n_gx, end_outer, 0)

    def opened(packed):
        both = packed.astype(jnp.float32)
        turned = pltpu.roll(both, rank, 1)
        return (
            jnp.where(low, both, turned).astype(jnp.bfloat16),
            jnp.where(low, turned, both).astype(jnp.bfloat16),
        )

    pairs = groups // 2

    def open_coarse(step, carry):
        for k in range(4 * pairs):
            first, second = opened(coarse_packed[step * 4 + k // pairs, k % pairs])
            index = step * 8 * pairs + 2 * k
            coarse[index] = first
            coarse[index + 1] = second
        return carry

    lax.fori_loop(0, total // 4, open_coarse, 0)
    loads[9].wait()

    def couple(blocks, store, pick, count):
        crossed = None
        for slot in range(0, count, 4):
            matrix = blocks(slot).reshape(4 * rank, rank)
            picked = jnp.concatenate([store[pick(slot + k)] for k in range(4)], axis=0)
            term = dot(picked[:, :rank], matrix, ROWS_BY_ROWS)
            crossed = term if crossed is None else crossed + term
        both = jnp.zeros((rhs, 2 * rank), jnp.float32)
        for k in range(0, 4, 2):
            lanes = slice(k * rank, (k + 2) * rank)
            upper = crossed[k * rhs : (k + 1) * rhs, lanes]
            lower = crossed[(k + 1) * rhs : (k + 2) * rhs, lanes]
            both = both + jnp.where(low, upper, lower)
        return both[:, :rank] + both[:, rank:]

    def one_group(group, carry):
        local1[group] = couple(
            lambda s: coarse_coupling_ref[group, pl.ds(s, 4)],
            coarse,
            lambda s: refs_ref[group, s],
            far1,
        ).astype(jnp.bfloat16)
        return carry

    lax.fori_loop(0, groups, one_group, 0, unroll=2)

    for group in range(groups):
        coupling_load(group).wait()

    def end_list(window, carry):
        @pl.when(in_window(window))
        def _():
            list_copy(window, window).wait_recv()
            list_copy(window, 2 * WINDOW - window).wait_send()

        for slot in range(half_slots):
            first, second = opened(listed_packed[window, slot])
            index = window * capacity + slot
            listed[index] = first
            listed[index + half_slots] = second
        return carry

    lax.fori_loop(0, WINDOWS, end_list, 0)

    def one_leaf(leaf, carry):
        local0 = couple(
            lambda s: coupling_ref[leaf, pl.ds(s, 4)],
            listed,
            lambda s: relay_ref[leaf, s],
            far0,
        )
        downward = dot(local1[leaf // CHILDREN], transfer_ref[leaf], ROWS_BY_ROWS)
        field = (local0 + downward).astype(jnp.bfloat16)
        span = pl.ds(pl.multiple_of(leaf * leaf_size, leaf_size), leaf_size)
        out_ref[:, span] = out_ref[:, span] + dot(field, basis_ref[leaf], PLAIN)
        return carry

    lax.fori_loop(0, leaf_count, one_leaf, 0, unroll=2)


def whole(sizes, tables, densities, points, weights, leaf_basis, transfer, coarse_coupling, coupling):
    rhs, columns = densities.shape
    leaf_count, rank, leaf_size = leaf_basis.shape
    total = sizes[0] * sizes[1]
    groups = leaf_count // CHILDREN
    capacity = tables[1].shape[0]
    anywhere = pl.BlockSpec(memory_space=pl.ANY)
    rim = REACH * leaf_size
    dma = pltpu.SemaphoreType.DMA
    operands = (densities, points, weights, leaf_basis, transfer, coarse_coupling, coupling)
    held = [pltpu.SMEM(x.shape, x.dtype) for x in tables]
    held += [pltpu.VMEM(x.shape, x.dtype) for x in operands]
    half = jnp.bfloat16
    return pl.pallas_call(
        functools.partial(whole_kernel, sizes),
        out_shape=jax.ShapeDtypeStruct((rhs, columns), jnp.float32),
        in_specs=[anywhere] * (len(tables) + len(operands)),
        out_specs=pl.BlockSpec(memory_space=pltpu.VMEM),
        scratch_shapes=held
        + [
            pltpu.VMEM((leaf_count, leaf_size, 48), half),
            pltpu.VMEM((leaf_count + 2 * REACH, 48, leaf_size), half),
            pltpu.VMEM((leaf_count + 2 * REACH, rhs, leaf_size), half),
            pltpu.VMEM((leaf_count, rhs, 2 * rank), half),
            pltpu.VMEM((WINDOWS, capacity // 2, rhs, 2 * rank), half),
            pltpu.VMEM((WINDOWS, capacity // 2, rhs, 2 * rank), half),
            pltpu.VMEM((total, groups // 2, rhs, 2 * rank), half),
            pltpu.VMEM((WINDOWS * capacity, rhs, 2 * rank), half),
            pltpu.VMEM((total * groups, rhs, 2 * rank), half),
            pltpu.VMEM((groups, rhs, rank), half),
            pltpu.VMEM((2, rhs, rim), half),
            pltpu.VMEM((2, 3, rim), jnp.float32),
            pltpu.VMEM((2, REACH, leaf_size), jnp.float32),
            dma((10,)),
            dma((groups,)),
            dma((2, 3)),
            dma((2, 3)),
            dma((WINDOWS,)),
            dma((WINDOWS,)),
            dma((sizes[1],)),
            dma((sizes[1],)),
            dma((sizes[0],)),
            dma((sizes[0],)),
        ],
        compiler_params=pltpu.CompilerParams(
            collective_id=0, has_side_effects=True, vmem_limit_bytes=63 * 1024 * 1024
        ),
        name="whole",
    )(*tables, *operands)


def local(
    sizes,
    densities,
    points,
    weights,
    near_offsets,
    leaf_basis,
    transfer,
    send_lists,
    relay_refs,
    leaf_coupling,
    coarse_refs,
    coarse_coupling,
):
    leaf_count, _, leaf_size = leaf_basis.shape
    lines = weights.reshape(leaf_count, leaf_size)
    tables = (near_offsets.T, send_lists[0].T, relay_refs, coarse_refs)
    return whole(
        sizes,
        tables,
        densities,
        points,
        lines,
        leaf_basis,
        transfer,
        coarse_coupling,
        leaf_coupling,
    )


def solution(mesh):
    sizes = (mesh.shape["gx"], mesh.shape["gy"])
    in_specs = (
        P(None, ("gx", "gy")),
        P(None, ("gx", "gy")),
        P(("gx", "gy")),
        P(("gx", "gy"), None),
        P(("gx", "gy"), None, None),
        P(("gx", "gy"), None, None),
        P(("gx", "gy"), None, None),
        P(("gx", "gy"), None),
        P(("gx", "gy"), None, None, None),
        P(("gx", "gy"), None),
        P(("gx", "gy"), None, None, None),
    )
    out_specs = P(None, ("gx", "gy"))
    return jax.shard_map(
        functools.partial(local, sizes),
        mesh=mesh,
        in_specs=in_specs,
        out_specs=out_specs,
        check_vma=False,
    )
```
